32 devices in a mesh: groups: 2 (over x), branch: 8 (over z, y), sub: 2 (over core).
Axes of the slice: x: 2, y: 2, z: 4, core: 2. Of those that a mesh axis runs over, the one named last changes fastest.
Arguments:
- right_sides: bfloat16 [32, 262144], P('groups', ('branch', 'sub')), parts along dimension 0, may hold values from -6 to 6
- near_blocks: bfloat16 [5, 64, 262144], P(None, None, ('branch', 'sub')), may hold values from -0.3125 to 0.3125
- near_leaves: int32 [4096, 5], P(('branch', 'sub')), may hold values from 0 to 4095, as said below
- leaf_basis: bfloat16 [32, 262144], P(None, ('branch', 'sub')), may hold values from -0.75 to 0.75
- transfer_first: bfloat16 [32, 32, 4096], P(None, None, ('branch', 'sub')), may hold values from -0.75 to 0.75
- transfer_second: bfloat16 [32, 32, 2048], P(None, None, ('branch', 'sub')), may hold values from -0.75 to 0.75
- transfer_third: bfloat16 [32, 32, 1024], P(None, None, ('branch', 'sub')), may hold values from -0.75 to 0.75
- coupling_first: bfloat16 [3, 32, 32, 2048], P(None, None, None, ('branch', 'sub')), may hold values from -0.625 to 0.625
- coupling_second: bfloat16 [3, 32, 32, 1024], P(None, None, None, ('branch', 'sub')), may hold values from -0.625 to 0.625
- list_first: int32 [2048, 3], P(('branch', 'sub')), may hold values from 0 to 2047, as said below
- list_second: int32 [1024, 3], P(('branch', 'sub')), may hold values from 0 to 1023, as said below
- top_coupling: bfloat16 [8, 32, 32, 512], P(None, None, None, ('branch', 'sub')), may hold values from -0.375 to 0.375
- top_nodes: int32 [512, 8], P(('branch', 'sub')), may hold values from 0 to 511
Outputs:
- first_image: bfloat16 [32, 262144], P('groups', ('branch', 'sub')), parts along dimension 0
- second_image: bfloat16 [32, 262144], P('groups', ('branch', 'sub')), parts along dimension 0
The draws below stay inside these ranges and needn't reach their ends.
There are 2 independent parts, one for each index of `groups`. The reference program is written for one: setup_inputs(seed, part) draws one part's arguments, and reference() takes and returns one part's arrays. A program takes and returns all parts, laid end to end along the dimension named above; an argument that names none is the same for every part. Nothing has to cross between parts.
Inputs may be any that keep to these rules, and one draw needn't show every extreme that they name: `near_leaves`: each entry is a leaf within 2 leaves of its row's leaf. `list_first`: each entry is a node within 2 nodes of its row's node. `list_second`: each entry is a node within 2 nodes of its row's node.
All inputs are finite; a program needn't handle non-finite values.
Results may differ from the reference program's by a relative error of at most 0.012.
Values may be sent and summed in bfloat16 or wider, within the bound.
No kernel may reach another device: no remote copies, remote signals or barrier semaphores. Data moves between devices by JAX's collectives and lax.ppermute only.
A program may use at most 192 MiB of HBM per device.

```python
import jax
import jax.numpy as jnp
from jax import lax

M = 64
K = 32
RHS = 16
NEAR = 5
NC = 3
NFAR = 8
HN = 2
HC = 2
LEAVES = 4096
ORDER = 262144
TOPN = 512


def banded_list(key, row_count, reach, leading, column_count):
    anchor = jnp.arange(row_count, dtype=jnp.int32)[:, None]
    chosen = jnp.broadcast_to(jnp.array(leading, dtype=jnp.int32)[None, :], (row_count, len(leading)))
    drawn = jax.random.randint(key, (row_count, column_count - len(leading)), -reach, reach + 1, dtype=jnp.int32)
    offsets = jnp.concatenate([chosen, drawn], axis=1)
    return jnp.clip(anchor + offsets, 0, row_count - 1).astype(jnp.int32)


def draw_near_leaves(key, part):
    key = jax.random.fold_in(key, 11)
    return banded_list(key, LEAVES, HN, (0, -HN, HN), NEAR)


def draw_list_first(key, part):
    key = jax.random.fold_in(key, 23)
    return banded_list(key, LEAVES // 2, HC, (-HC, HC), NC)


def draw_list_second(key, part):
    key = jax.random.fold_in(key, 37)
    return banded_list(key, LEAVES // 4, HC, (-HC, HC), NC)


def with_ends(values, key, low, top_value):
    shape = values.shape
    place = [jax.random.randint(jax.random.fold_in(key, axis), (), 0, shape[axis]) for axis in range(len(shape))]
    values = values.at[tuple(place)].set(low)
    longest = shape.index(max(shape))
    place[longest] = (place[longest] + 1) % shape[longest]
    return values.at[tuple(place)].set(top_value)


def shard_levels(stream_key, dims, shards, least, top_value):
    factor_of, own = 1.0, jax.random.fold_in(stream_key, 6)
    for position, parts in shards:
        draws = jnp.exp(jax.random.uniform(jax.random.fold_in(own, position), (parts,), jnp.float32, least / len(shards), top_value / len(shards)))
        factor_of = factor_of * jnp.repeat(draws, dims[position] // parts).reshape([-1 if axis == position else 1 for axis in range(len(dims))])
    return factor_of


def normal_values(own_key, dims, width, bound, shards=(), kind=jnp.bfloat16):
    level = shard_levels(own_key, dims, shards, -0.22, 0.18) if shards else 1.0
    result = jax.random.normal(own_key, dims, jnp.float32) * width * level
    return jnp.minimum(jnp.maximum(result, -bound), bound).astype(kind)


def setup_inputs(seed: int = 0, part: int = 0) -> dict:
    keys = jax.random.split(jax.random.key(seed), 14)
    own_keys = jax.random.split(jax.random.fold_in(keys[13], part), 14)
    right_sides = normal_values(own_keys[0], (RHS, ORDER), 1.0, 6.0, ((1, 16),))
    near_blocks = normal_values(keys[1], (NEAR, M, ORDER), (NEAR * M) ** -0.5, 0.3125, ((2, 16),))
    near_leaves = draw_near_leaves(jax.random.fold_in(keys[13], 71), part)
    leaf_basis = normal_values(keys[3], (K, ORDER), M ** -0.5, 0.75, ((1, 16),))
    transfer_first = normal_values(keys[4], (K, K, LEAVES), (2 * K) ** -0.5, 0.75, ((2, 16),))
    transfer_second = normal_values(keys[5], (K, K, LEAVES // 2), (2 * K) ** -0.5, 0.75, ((2, 16),))
    transfer_third = normal_values(keys[6], (K, K, LEAVES // 4), (2 * K) ** -0.5, 0.75, ((2, 16),))
    coupling_first = normal_values(keys[7], (NC, K, K, LEAVES // 2), (NC * K) ** -0.5, 0.625, ((3, 16),))
    coupling_second = normal_values(keys[8], (NC, K, K, LEAVES // 4), (NC * K) ** -0.5, 0.625, ((3, 16),))
    list_first = draw_list_first(jax.random.fold_in(keys[13], 71), part)
    list_second = draw_list_second(jax.random.fold_in(keys[13], 71), part)
    top_coupling = normal_values(keys[11], (NFAR, K, K, TOPN), (NFAR * K) ** -0.5, 0.375, ((3, 16),))
    top_nodes = with_ends(jax.random.randint(keys[12], (TOPN, NFAR), 0, TOPN), jax.random.fold_in(keys[12], 1), 0, TOPN - 1).astype(jnp.int32)
    return {"right_sides": right_sides, "near_blocks": near_blocks, "near_leaves": near_leaves, "leaf_basis": leaf_basis, "transfer_first": transfer_first, "transfer_second": transfer_second, "transfer_third": transfer_third, "coupling_first": coupling_first, "coupling_second": coupling_second, "list_first": list_first, "list_second": list_second, "top_coupling": top_coupling, "top_nodes": top_nodes}


def upward(lower, transfer):
    rhs_count, rank, node_count = lower.shape
    paired = lower.astype(jnp.float32).reshape(rhs_count, rank, node_count // 2, 2)
    matrices = transfer.astype(jnp.float32).reshape(rank, rank, node_count // 2, 2)
    return jnp.einsum('kmps,rkps->rmp', matrices, paired, precision=lax.Precision.HIGHEST).astype(jnp.bfloat16)


def couple(coefs, columns, coupling):
    picked = coefs[:, :, columns].astype(jnp.float32)
    return jnp.einsum('jkmi,rkij->rmi', coupling.astype(jnp.float32), picked, precision=lax.Precision.HIGHEST)


def downward(partial_value, upper, transfer):
    spread = jnp.repeat(upper.astype(jnp.float32), 2, axis=2)
    term = jnp.einsum('kmc,rmc->rkc', transfer.astype(jnp.float32), spread, precision=lax.Precision.HIGHEST)
    return (partial_value + term).astype(jnp.bfloat16)


def apply_matrix(vectors, near_blocks, near_leaves, leaf_basis, transfer_first, transfer_second, transfer_third,
                 coupling_first, coupling_second, list_first, list_second, top_coupling, top_nodes):
    rhs_count, order = vectors.shape
    leaf_count = order // M
    grid = vectors.reshape(rhs_count, leaf_count, M)
    picked = grid[:, near_leaves].astype(jnp.float32)
    blocks = near_blocks.astype(jnp.float32).reshape(NEAR, M, leaf_count, M)
    near_part = jnp.einsum('jbla,rljb->rla', blocks, picked, precision=lax.Precision.HIGHEST)
    basis = leaf_basis.astype(jnp.float32).reshape(K, leaf_count, M)
    coef_leaf = jnp.einsum('kla,rla->rkl', basis, grid.astype(jnp.float32), precision=lax.Precision.HIGHEST).astype(jnp.bfloat16)
    coef_first = upward(coef_leaf, transfer_first)
    coef_second = upward(coef_first, transfer_second)
    coef_third = upward(coef_second, transfer_third)
    far_first = couple(coef_first, list_first, coupling_first)
    far_second = couple(coef_second, list_second, coupling_second)
    far_third = couple(coef_third, top_nodes, top_coupling)
    down_third = far_third.astype(jnp.bfloat16)
    down_second = downward(far_second, down_third, transfer_third)
    down_first = downward(far_first, down_second, transfer_second)
    down_leaf = downward(jnp.float32(0.0), down_first, transfer_first)
    far_part = jnp.einsum('kla,rkl->rla', basis, down_leaf.astype(jnp.float32), precision=lax.Precision.HIGHEST)
    return (near_part + far_part).reshape(rhs_count, order).astype(jnp.bfloat16)


def reference(right_sides, near_blocks, near_leaves, leaf_basis, transfer_first, transfer_second, transfer_third,
              coupling_first, coupling_second, list_first, list_second, top_coupling, top_nodes):
    tables = (near_blocks, near_leaves, leaf_basis, transfer_first, transfer_second, transfer_third,
              coupling_first, coupling_second, list_first, list_second, top_coupling, top_nodes)
    first_image = apply_matrix(right_sides, *tables)
    second_image = apply_matrix(first_image, *tables)
    return (first_image, second_image)
```

```python
import functools

import jax
import jax.numpy as jnp
from jax import lax
from jax.experimental import pallas as pl
from jax.experimental.pallas import tpu as pltpu
from jax.sharding import PartitionSpec as P

M = 64
K = 32
NEAR = 5
NC = 3
NFAR = 8
HN = 2
HC = 2
LANES = 128
AXES = ("branch", "sub")
PIECES = 3
CHUNK = 1024
F32 = jnp.float32
BF16 = jnp.bfloat16
NT = (((1,), (1,)), ((), ()))


def iota(shape, dim):
    return lax.broadcasted_iota(jnp.int32, shape, dim)


def place(node, count, levels):
    where = jnp.zeros_like(node)
    for level in range(levels):
        count //= 2
        where = where + (node & 1) * count
        node = node >> 1
    return where + node


def place_static(node, count, levels):
    where = 0
    for level in range(levels):
        count //= 2
        where += (node & 1) * count
        node >>= 1
    return where + node


def lane_order(count, levels, copies=1):
    rows = place(iota((count, count * copies), 0), count, levels)
    columns = iota((count, count * copies), 1) & (count - 1)
    return jnp.where(rows == columns, 1.0, 0.0).astype(BF16)


def dot(a, b):
    return jnp.dot(a, b, preferred_element_type=F32)


def rounded(x):
    return x.astype(BF16).astype(F32)


def contract(terms, init, lanes):
    def step(position, accs):
        for matrix_at, x_at in terms:
            matrix = matrix_at(position).astype(F32)
            accs = tuple(acc + matrix * x_at(r, position) for r, acc in enumerate(accs))
        return accs

    return lax.fori_loop(0, K, step, init, unroll=4)


def prep_up_kernel(first_ref, second_ref, third_ref, up1_ref, up2_ref, up3_ref):
    for source, target, levels, copies in ((first_ref, up1_ref, 3, 1), (second_ref, up2_ref, 2, 1), (third_ref, up3_ref, 1, 2)):
        count = source.shape[2]
        order = lane_order(count, levels, copies)
        for k in range(0, K, 4):
            rows = source[k : k + 4].reshape(4 * K, count)
            target[k : k + 4] = dot(rows, order).astype(BF16).reshape(4, K, count * copies)


def prep_rest_kernel(up1_ref, up2_ref, up3_ref, c1_ref, c2_ref, c3_ref, d1_ref, d2_ref, d3_ref, m1_ref, m2_ref, m3_ref, wide_ref):
    for source, target in ((up1_ref, d1_ref), (up2_ref, d2_ref), (up3_ref, d3_ref)):
        for tile in range(source.shape[2] // LANES):
            lanes = slice(tile * LANES, (tile + 1) * LANES)
            wide_ref[...] = source[:, :, lanes].astype(F32).reshape(K * K, LANES)
            for m in range(K):
                target[m, :, lanes] = wide_ref[pl.ds(m, K, stride=K), :].astype(BF16)
    for source, target, levels, copies in ((c1_ref, m1_ref, 2, 1), (c2_ref, m2_ref, 1, 2)):
        count = source.shape[3]
        order = lane_order(count, levels, copies)
        for j in range(NC):
            for k in range(0, K, 8):
                rows = source[j, k : k + 8].reshape(8 * K, count)
                target[j, k : k + 8] = dot(rows, order).astype(BF16).reshape(8, K, LANES)
    top = c3_ref.shape[3]
    group = LANES // top
    for h in range(NFAR // group):
        for k in range(0, K, 8):
            total = None
            for q in range(group):
                put = jnp.where(iota((top, LANES), 0) + q * top == iota((top, LANES), 1), 1.0, 0.0).astype(BF16)
                part = dot(c3_ref[h * group + q, k : k + 8].reshape(8 * K, top), put)
                total = part if total is None else total + part
            m3_ref[h, k : k + 8] = total.astype(BF16).reshape(8, K, LANES)


def up_kernel(z_ref, basis_ref, up1_ref, up2_ref, up3_ref, sent_ref, coef1_ref, coef2_ref, rows_ref, x0_ref, x1_ref, x2_ref):
    rhs, order = z_ref.shape
    leaves = order // M
    top = leaves // 8
    low = iota((rhs, LANES), 1) < M
    zero = jnp.zeros((rhs, LANES), BF16)

    @pl.loop(0, leaves // 16)
    def _(outer):
        for inner in range(4):
            chunk = outer * 4 + inner
            lanes = pl.ds(pl.multiple_of(chunk * 256, 256), 256)
            z = z_ref[:, lanes]
            left, right = z[:, :LANES], z[:, LANES:]
            none = jnp.zeros_like(left)
            masked = jnp.concatenate(
                [
                    jnp.concatenate([jnp.where(low, left, none), none], axis=1),
                    jnp.concatenate([jnp.where(low, none, left), none], axis=1),
                    jnp.concatenate([none, jnp.where(low, right, none)], axis=1),
                    jnp.concatenate([none, jnp.where(low, none, right)], axis=1),
                ],
                axis=0,
            )
            coef = lax.dot_general(masked, basis_ref[:, lanes], NT, preferred_element_type=F32)
            rows_ref[pl.ds(pl.multiple_of(chunk * 64, 64), 64), :K] = coef

    unit = jnp.where(iota((K, K), 0) == iota((K, K), 1), 1.0, 0.0).astype(BF16)
    for r in range(rhs):
        pieces = []
        for c in range(2):
            for b in range(2):
                for a in range(2):
                    pieces.append(rows_ref[pl.ds(rhs * (4 * a + 2 * b + c) + r, top, stride=8 * rhs), :K])
        tall = jnp.concatenate(pieces, axis=0).astype(BF16)
        wide = lax.dot_general(unit, tall, NT, preferred_element_type=F32)
        x0_ref[0, r] = wide[:, :LANES]
        x0_ref[1, r] = wide[:, LANES:]

    half = rhs // 2
    zeros = tuple(jnp.zeros((K, LANES), F32) for _ in range(half))
    for first in (0, half):
        terms = [
            (
                functools.partial(lambda s, k: up1_ref[k, :, s * LANES : (s + 1) * LANES], s),
                functools.partial(lambda s, r, k: x0_ref[s, first + r, pl.ds(k, 1), :], s),
            )
            for s in range(2)
        ]
        for r, acc in enumerate(contract(terms, zeros, LANES)):
            coef1_ref[first + r] = acc.astype(BF16)
            x1_ref[first + r] = rounded(acc)
    low = iota((K, LANES), 1) < M
    for first in (0, half):
        terms = [(lambda k: up2_ref[k], lambda r, k: x1_ref[first + r, pl.ds(k, 1), :])]
        for r, acc in enumerate(contract(terms, zeros, LANES)):
            total = rounded(acc + pltpu.roll(acc, 64, 1))
            if first == 0:
                x2_ref[r] = total
            else:
                both = jnp.where(low, x2_ref[r], total)
                x2_ref[r] = both
                coef2_ref[r] = both.astype(BF16)
    terms = [(lambda k: up3_ref[k], lambda r, k: x2_ref[r, pl.ds(k, 1), :])]
    sums = [acc + pltpu.roll(acc, 32, 1) for acc in contract(terms, zeros, LANES)]
    odd = (iota((K, LANES), 1) & 32) > 0
    for r in range(half // 2):
        sent_ref[r * K : (r + 1) * K] = jnp.where(odd, sums[r], pltpu.roll(sums[r + half // 2], 96, 1)).astype(BF16)

    def ends(count, offset, shift):
        row, column = iota((LANES, LANES), 0), iota((LANES, LANES), 1)
        hit = (row == -1)
        for copy in range(LANES // count):
            for e, node in enumerate((0, 1, count - 2, count - 1)):
                at = place_static(node, count, 2 if count == LANES else 1)
                hit = hit | ((row == copy * count + at) & (column == copy * M + offset + e))
        return jnp.where(hit, 1.0, 0.0).astype(BF16)

    first_ends = dot(x1_ref[...].astype(BF16).reshape(rhs * K, LANES), ends(LANES, 0, 0)).reshape(rhs, K, LANES)
    second_ends = dot(x2_ref[...].astype(BF16).reshape(half * K, LANES), ends(M, 4, 64)).reshape(half, K, LANES)
    packed = jnp.zeros((K, LANES), F32)
    for r in range(rhs):
        value = first_ends[r]
        if r < half:
            value = value + second_ends[r]
        packed = packed + (pltpu.roll(value, 8 * r, 1) if r else value)
    base = half // 2 * K
    sent_ref[base : base + K] = packed.astype(BF16)
    sent_ref[base + K : base + K + rhs] = z_ref[:, :LANES]
    sent_ref[base + K + rhs : base + K + 2 * rhs] = z_ref[:, order - LANES :]


def put_leaves(target_ref, tile, slot):
    low = iota(tile.shape, 1) < M
    wide = tile.astype(F32)
    swapped = pltpu.roll(wide, M, 1)
    target_ref[slot] = jnp.where(low, wide, swapped).astype(BF16)
    target_ref[slot + 1] = jnp.where(low, swapped, wide).astype(BF16)


def own_blocks(res, rhs):
    low = iota((rhs, LANES), 1) < M
    return jnp.concatenate(
        [
            jnp.where(low, res[:rhs, :LANES], res[rhs : 2 * rhs, :LANES]),
            jnp.where(low, res[2 * rhs : 3 * rhs, LANES:], res[3 * rhs :, LANES:]),
        ],
        axis=1,
    )


def near_group(read, weights, rhs):
    low = iota((rhs, LANES), 1) < M
    rows = []
    for leaf in range(4):
        z = [read(j, leaf) for j in range(NEAR)]
        rows.append(jnp.concatenate([jnp.where(low, z[0], z[1]), jnp.where(low, z[2], z[3]), z[4][:, :M]], axis=1))
    return own_blocks(dot(jnp.concatenate(rows, axis=0), weights), rhs)


def near_kernel(chunk0, leaves_ref, z_ref, blocks_hbm, out_ref, z_leaves_ref, blocks_ref, sems):
    rhs, order = z_ref.shape
    chunks = out_ref.shape[1] // CHUNK

    def copy(c):
        there = pl.ds(pl.multiple_of((chunk0 + c) * CHUNK, CHUNK), CHUNK)
        here = pl.ds(pl.multiple_of(c * CHUNK, CHUNK), CHUNK)
        return pltpu.make_async_copy(blocks_hbm.at[:, :, there], blocks_ref.at[:, :, here], sems.at[c])

    for c in range(chunks):
        copy(c).start()
    per = CHUNK // M
    first_tile = max(chunk0 * (CHUNK // LANES) - 1, 0)
    last_tile = min((chunk0 + chunks) * (CHUNK // LANES) + 1, order // LANES)
    for t in range(first_tile, last_tile):
        put_leaves(z_leaves_ref, z_ref[:, t * LANES : (t + 1) * LANES], 2 * t + HN)

    @pl.loop(0, chunks)
    def _(c):
        copy(c).wait()
        for g in range(CHUNK // 256):
            leaf0 = (chunk0 + c) * per + 4 * g
            lanes = pl.ds(pl.multiple_of(c * CHUNK + g * 256, 256), 256)
            weights = blocks_ref[:, :, lanes].reshape(NEAR * M, 256)
            out_ref[:, lanes] = near_group(lambda j, e: z_leaves_ref[leaves_ref[j, leaf0 + e]], weights, rhs)


def bit_reverse(value, bits):
    out = jnp.zeros_like(value)
    for b in range(bits):
        out = out + (((value >> b) & 1) << (bits - 1 - b))
    return out


def list_rows(nodes, me, count, halo0):
    local = nodes - me * count
    inside = place(jnp.clip(local, 0, count - 1), count, 2 if count == LANES else 1)
    left = halo0 + 4 + local
    right = halo0 + local - count
    return jnp.where(local < 0, left, jnp.where(local >= count, right, inside))


def in_order(rows, count, levels):
    wide = jnp.concatenate([rows.astype(F32)] + [jnp.zeros((8 - rows.shape[0], count), F32)], axis=0).astype(BF16)
    return dot(wide, lane_order(count, levels)).astype(jnp.int32)


def down_kernel(
    bits, me_ref, leaves_ref, early_ref, late_ref, coef1_ref, coef2_ref, z_ref, *refs
):
    near_refs = refs[:PIECES]
    (head_ref, tail_ref, basis_ref, list1_ref, list2_ref, top_ref, m1_ref, m2_ref, m3_ref, d1_ref, d2_ref, d3_ref,
     out_ref, every_ref, picks_ref, far1_ref, x_ref, x0_ref, rows_ref, z_leaves_ref) = refs[PIECES:]
    rhs, order = z_ref.shape
    leaves = order // M
    top = leaves // 8
    half = rhs // 2
    me = me_ref[0]
    devices = 1 << bits
    own_rows = half // 2 * K

    def block(device, rows):
        at = bit_reverse(jnp.bitwise_xor(device, me), bits)
        early = early_ref[jnp.minimum(at, devices // 2 - 1), rows]
        late = late_ref[jnp.maximum(at - devices // 2, 0), rows]
        return jnp.where(at < devices // 2, early.astype(F32), late.astype(F32))

    before = jnp.maximum(me - 1, 0)
    after = jnp.minimum(me + 1, devices - 1)

    z_before = block(before, slice(own_rows + K + rhs, own_rows + K + 2 * rhs)).astype(BF16)
    z_after = block(after, slice(own_rows + K, own_rows + K + rhs)).astype(BF16)
    put_leaves(z_leaves_ref, z_before, 0)
    for t in range(3):
        put_leaves(z_leaves_ref, z_ref[:, t * LANES : (t + 1) * LANES], 2 + 2 * t)
        put_leaves(z_leaves_ref, z_ref[:, order - (3 - t) * LANES : order - (2 - t) * LANES or None], 8 + 2 * t)
    put_leaves(z_leaves_ref, z_after, 14)
    head = near_group(lambda j, e: z_leaves_ref[leaves_ref[j, e]], head_ref[...].reshape(NEAR * M, 256), rhs)
    skip = leaves + 2 * HN - 16
    tail = near_group(
        lambda j, e: z_leaves_ref[leaves_ref[j, leaves - 4 + e] - skip], tail_ref[...].reshape(NEAR * M, 256), rhs
    )

    sides = slice(own_rows, own_rows + K)
    halo = jnp.where((iota((K, LANES), 1) & 2) > 0, block(before, sides), block(after, sides))

    group = iota((own_rows, LANES), 1) // top
    per = LANES // top
    for tile in range(devices // per):
        source = early_ref if tile < devices // per // 2 else late_ref
        first = tile * per - (0 if tile < devices // per // 2 else devices // 2)
        parts = [source[first + q, :own_rows].astype(F32) for q in range(per)]
        for g in range(per):
            merged = None
            for q in range(per):
                shift = (q - g) * top % LANES
                moved = pltpu.roll(parts[q], shift, 1) if shift else parts[q]
                merged = moved if merged is None else jnp.where(group == q, moved, merged)
            every_ref[g * own_rows : (g + 1) * own_rows, tile * LANES : (tile + 1) * LANES] = merged.astype(BF16)
    nodes = top_ref[...]
    rows = bit_reverse(jnp.bitwise_xor(nodes // top, me), bits) * top + nodes % top
    hot = []
    for j in range(NFAR):
        hot.append(jnp.where(iota((devices * top, top), 0) == rows[j : j + 1], 1.0, 0.0).astype(BF16))
    for h in range(NFAR // per):
        wide = None
        for q in range(per):
            put = jnp.where(iota((top, LANES), 0) + q * top == iota((top, LANES), 1), 1.0, 0.0).astype(BF16)
            part = dot(hot[h * per + q], put)
            wide = part if wide is None else wide + part
        picked = dot(every_ref[...], wide.astype(BF16))
        picks_ref[:, h * K : (h + 1) * K, :] = picked.reshape(rhs, K, LANES)
    zeros = tuple(jnp.zeros((K, LANES), F32) for _ in range(half))
    groups_of = [1, 0, 3, 2]

    def slot(r):
        quarter = rhs // 4
        return groups_of[r // quarter] * quarter + r % quarter

    low = iota((K, LANES), 1) < M
    kept = {}
    for first in range(0, rhs, half):
        terms = [
            (
                functools.partial(lambda h, k: m3_ref[h, k], h),
                functools.partial(lambda h, r, k: picks_ref[slot(first + r), pl.ds(h * K + k, 1), :], h),
            )
            for h in range(NFAR // per)
        ]
        for r, acc in enumerate(contract(terms, zeros, LANES)):
            acc = acc + pltpu.roll(acc, 64, 1)
            acc = rounded(acc + pltpu.roll(acc, 32, 1))
            if first == 0:
                x_ref[r] = acc
            else:
                x_ref[r] = jnp.where(low, x_ref[r], acc)

    rows = in_order(list_rows(list2_ref[...], me, M, 4), M, 1)
    hot = []
    for j in range(NC):
        row = jnp.concatenate([rows[j : j + 1], rows[j : j + 1]], axis=1)
        column_half = (iota((LANES, LANES), 1) // M) * M
        index = iota((LANES, LANES), 0) - column_half
        hot.append((row, index))
    local = list2_ref[...] - me * M
    outside = in_order(jnp.where((local < 0) | (local >= M), 1, 0), M, 1)
    tables = []
    for j in range(NC):
        row, index = hot[j]
        out = jnp.concatenate([outside[j : j + 1], outside[j : j + 1]], axis=1)
        own = jnp.where((row == index) & (out == 0), 1.0, 0.0)
        far = jnp.where((row == index) & (out == 1), 1.0, 0.0)
        tables.append(jnp.concatenate([own, far], axis=0).astype(BF16))
    table = jnp.concatenate(tables, axis=1)
    for r in range(half):
        turned = pltpu.roll(halo, LANES - 8 * r, 1) if r else halo
        picked = dot(jnp.concatenate([coef2_ref[r], turned.astype(BF16)], axis=1), table)
        for j in range(NC):
            picks_ref[r, j * K : (j + 1) * K, :] = picked[:, j * LANES : (j + 1) * LANES]
    terms = [
        (
            functools.partial(lambda j, k: m2_ref[j, k], j),
            functools.partial(lambda j, r, k: picks_ref[r, pl.ds(j * K + k, 1), :], j),
        )
        for j in range(NC)
    ] + [(lambda m: d3_ref[m], lambda r, m: x_ref[r, pl.ds(m, 1), :])]
    second = [rounded(acc) for acc in contract(terms, zeros, LANES)]
    for r, value in enumerate(second):
        swapped = pltpu.roll(value, M, 1)
        x_ref[r] = jnp.where(low, value, swapped)
        x_ref[r + half] = jnp.where(low, swapped, value)

    rows = in_order(list_rows(list1_ref[...], me, LANES, LANES), LANES, 2)
    table = jnp.concatenate(
        [jnp.where(iota((2 * LANES, LANES), 0) == rows[j : j + 1], 1.0, 0.0) for j in range(NC)], axis=1
    ).astype(BF16)
    for r in range(rhs):
        turned = pltpu.roll(halo, LANES - 8 * r, 1) if r else halo
        picked = dot(jnp.concatenate([coef1_ref[r], turned.astype(BF16)], axis=1), table)
        for j in range(NC):
            picks_ref[r, j * K : (j + 1) * K, :] = picked[:, j * LANES : (j + 1) * LANES]
    for first in (0, half):
        terms = [
            (
                functools.partial(lambda j, k: m1_ref[j, k], j),
                functools.partial(lambda j, r, k: picks_ref[first + r, pl.ds(j * K + k, 1), :], j),
            )
            for j in range(NC)
        ] + [(lambda m: d2_ref[m], lambda r, m: x_ref[first + r, pl.ds(m, 1), :])]
        for r, acc in enumerate(contract(terms, zeros, LANES)):
            far1_ref[first + r] = rounded(acc)

    for first in (0, half):
        for s in range(2):
            lanes = slice(s * LANES, (s + 1) * LANES)
            terms = [(lambda m: d1_ref[m, :, lanes], lambda r, m: far1_ref[first + r, pl.ds(m, 1), :])]
            for r, acc in enumerate(contract(terms, zeros, LANES)):
                x0_ref[s, first + r] = acc
    unit = jnp.where(iota((leaves, leaves), 0) == iota((leaves, leaves), 1), 1.0, 0.0).astype(BF16)
    for r in range(rhs):
        tall = lax.dot_general(unit, jnp.concatenate([x0_ref[0, r], x0_ref[1, r]], axis=1).astype(BF16), NT, preferred_element_type=F32)
        at = 0
        for c in range(2):
            for b in range(2):
                for a in range(2):
                    rows_ref[pl.ds(rhs * (4 * a + 2 * b + c) + r, top, stride=8 * rhs), :K] = tall[at : at + top]
                    at += top
    chunk = 0
    for piece in range(PIECES):
        count = near_refs[piece].shape[1] // 256

        def leaf_group(g, near_value):
            lanes = pl.ds(pl.multiple_of(g * 256, 256), 256)
            coefs = rows_ref[pl.ds(pl.multiple_of(g * 64, 64), 64), :K].astype(BF16)
            far = own_blocks(dot(coefs, basis_ref[:, lanes]), rhs)
            out_ref[:, lanes] = (near_value + far).astype(BF16)

        start, stop = 0, count
        if piece == 0:
            leaf_group(0, head)
            start = 4
            for g in range(1, 4):
                leaf_group(chunk + g, near_refs[piece][:, g * 256 : (g + 1) * 256])
        if piece == PIECES - 1:
            stop = count - 4
            for g in range(stop, count - 1):
                leaf_group(chunk + g, near_refs[piece][:, g * 256 : (g + 1) * 256])
            leaf_group(chunk + count - 1, tail)

        @pl.loop(start // 4, stop // 4)
        def _(outer):
            for inner in range(4):
                g = outer * 4 + inner
                lanes = pl.ds(pl.multiple_of(g * 256, 256), 256)
                leaf_group(chunk + g, near_refs[piece][:, lanes])

        chunk += count


VM = pl.BlockSpec(memory_space=pltpu.VMEM)
SM = pl.BlockSpec(memory_space=pltpu.SMEM)
HBM = pl.BlockSpec(memory_space=pl.ANY)
PARAMS = pltpu.CompilerParams(vmem_limit_bytes=56 * 2**20)


def cost(flops, moved):
    return pl.CostEstimate(flops=flops, bytes_accessed=moved, transcendentals=0)


def shape(dims, kind=BF16):
    return jax.ShapeDtypeStruct(dims, kind)


def body(
    right_sides, near_blocks, near_leaves, leaf_basis, transfer_first, transfer_second, transfer_third,
    coupling_first, coupling_second, list_first, list_second, top_coupling, top_nodes,
):
    position = lax.axis_index(AXES)
    devices = lax.axis_size("branch") * lax.axis_size("sub")
    bits = devices.bit_length() - 1
    rhs, order = right_sides.shape
    leaves = order // M
    half = rhs // 2
    me = position.astype(jnp.int32).reshape(1)
    near_local = near_leaves.T - (position * leaves - HN)
    lists = (list_first.T, list_second.T, top_nodes.T)

    ups = pl.pallas_call(
        prep_up_kernel,
        out_shape=(shape((K, K, leaves)), shape((K, K, LANES)), shape((K, K, LANES))),
        in_specs=[VM] * 3,
        out_specs=(VM,) * 3,
        compiler_params=PARAMS,
    )(transfer_first, transfer_second, transfer_third)
    downs = pl.pallas_call(
        prep_rest_kernel,
        out_shape=(
            shape((K, K, leaves)), shape((K, K, LANES)), shape((K, K, LANES)),
            shape((NC, K, K, LANES)), shape((NC, K, K, LANES)), shape((NFAR * top_coupling.shape[3] // LANES, K, K, LANES)),
        ),
        in_specs=[VM] * 6,
        out_specs=(VM,) * 6,
        scratch_shapes=[pltpu.VMEM((K * K, LANES), F32)],
        compiler_params=PARAMS,
        cost_estimate=cost(10**9, 9 * 2**20),
    )(*ups, coupling_first, coupling_second, top_coupling)
    d1, d2, d3, m1, m2, m3 = downs
    sent_rows = half // 2 * K + K + 2 * rhs
    chunks = order // CHUNK
    cuts = [chunks * i // PIECES for i in range(PIECES + 1)]

    def product(vectors):
        sent, coef1, coef2 = pl.pallas_call(
            up_kernel,
            out_shape=(shape((sent_rows, LANES)), shape((rhs, K, LANES)), shape((half, K, LANES))),
            in_specs=[VM] * 5,
            out_specs=(VM,) * 3,
            scratch_shapes=[
                pltpu.VMEM((leaves * rhs, LANES), F32),
                pltpu.VMEM((leaves // LANES, rhs, K, LANES), F32),
                pltpu.VMEM((rhs, K, LANES), F32),
                pltpu.VMEM((half, K, LANES), F32),
            ],
            compiler_params=PARAMS,
            cost_estimate=cost(10**8, 3 * 2**20),
        )(vectors, leaf_basis, *ups)
        nears = []
        for i in range(PIECES):
            count = cuts[i + 1] - cuts[i]
            nears.append(
                pl.pallas_call(
                    functools.partial(near_kernel, cuts[i]),
                    out_shape=shape((rhs, count * CHUNK), F32),
                    in_specs=[SM, VM, HBM],
                    out_specs=VM,
                    scratch_shapes=[
                        pltpu.VMEM((leaves + 2 * HN, rhs, LANES), BF16),
                        pltpu.VMEM((NEAR, M, count * CHUNK), BF16),
                        pltpu.SemaphoreType.DMA((count,)),
                    ],
                    compiler_params=PARAMS,
                    cost_estimate=cost(10**9, 8 * 2**20),
                )(near_local, vectors, near_blocks)
            )
        every = sent[None]
        for b in reversed(range(bits)):
            pairs = [(i, i ^ (1 << b)) for i in range(devices)]
            other = lax.ppermute(every, AXES, pairs)
            if b:
                every = jnp.concatenate([every, other], axis=0)
        return pl.pallas_call(
            functools.partial(down_kernel, bits),
            grid=(1,),
            out_shape=shape((rhs, order)),
            in_specs=[SM, SM] + [VM] * 5 + [VM] * PIECES
            + [
                pl.BlockSpec((NEAR, M, 256), lambda i: (0, 0, 0)),
                pl.BlockSpec((NEAR, M, 256), lambda i: (0, 0, order // 256 - 1)),
            ]
            + [VM] * 10,
            out_specs=VM,
            scratch_shapes=[
                pltpu.VMEM((rhs * K, devices * (leaves // 8)), BF16),
                pltpu.VMEM((rhs, NC * K, LANES), F32),
                pltpu.VMEM((rhs, K, LANES), F32),
                pltpu.VMEM((rhs, K, LANES), F32),
                pltpu.VMEM((leaves // LANES, rhs, K, LANES), F32),
                pltpu.VMEM((leaves * rhs, LANES), F32),
                pltpu.VMEM((16, rhs, LANES), BF16),
            ],
            compiler_params=PARAMS,
            cost_estimate=cost(10**9, 8 * 2**20),
        )(me, near_local, every, other, coef1, coef2, vectors, *nears, near_blocks, near_blocks, leaf_basis,
          *lists, m1, m2, m3, d1, d2, d3)

    first_image = product(right_sides)
    second_image = product(first_image)
    return (first_image, second_image)


def solution(mesh):
    tree = P(None, None, AXES)
    placed = (
        P("groups", AXES), tree, P(AXES, None), P(None, AXES), tree, tree, tree,
        P(None, None, None, AXES), P(None, None, None, AXES), P(AXES, None), P(AXES, None),
        P(None, None, None, AXES), P(AXES, None),
    )
    return jax.shard_map(
        body, mesh=mesh, in_specs=placed, out_specs=(P("groups", AXES), P("groups", AXES)), check_vma=False
    )
```

```python
import functools

import jax
import jax.numpy as jnp
from jax import lax
from jax.experimental import pallas as pl
from jax.experimental.pallas import tpu as pltpu
from jax.sharding import PartitionSpec as P

M = 64
K = 32
NEAR = 5
NC = 3
NFAR = 8
HN = 2
HC = 2
LANES = 128
AXES = ("branch", "sub")
PIECES = 2
GROUPS = 64
UNROLL = 32
FIRST = 1
BATCH = 4
CHUNK = 1024
F32 = jnp.float32
BF16 = jnp.bfloat16
NT = (((1,), (1,)), ((), ()))


def iota(shape, dim):
    return lax.broadcasted_iota(jnp.int32, shape, dim)


def place(node, count, levels):
    where = jnp.zeros_like(node)
    for level in range(levels):
        count //= 2
        where = where + (node & 1) * count
        node = node >> 1
    return where + node


def place_static(node, count, levels):
    where = 0
    for level in range(levels):
        count //= 2
        where += (node & 1) * count
        node >>= 1
    return where + node


def lane_order(count, levels, copies=1):
    rows = place(iota((count, count * copies), 0), count, levels)
    columns = iota((count, count * copies), 1) & (count - 1)
    return jnp.where(rows == columns, 1.0, 0.0).astype(BF16)


def dot(a, b):
    return jnp.dot(a, b, preferred_element_type=F32)


def end_nodes(count):
    return (0, 1, count - 2, count - 1)


def end_columns(count, offset):
    row, lane = iota((count, LANES), 0), iota((count, LANES), 1) & 7
    hit = row < 0
    for e, node in enumerate(end_nodes(count)):
        hit = hit | ((row == node) & (lane == offset + e))
    return jnp.where(hit, 1.0, 0.0).astype(BF16)


def rounded(x):
    return x.astype(BF16).astype(F32)


def contract(terms, init, lanes):
    def step(position, accs):
        for matrix_at, x_at in terms:
            matrix = matrix_at(position).astype(F32)
            accs = tuple(acc + matrix * x_at(r, position) for r, acc in enumerate(accs))
        return accs

    return lax.fori_loop(0, K, step, init, unroll=UNROLL)


def prep_up_kernel(first_ref, second_ref, third_ref, up1_ref, up2_ref, up3_ref):
    for source, target, levels, copies in ((first_ref, up1_ref, 3, 1), (second_ref, up2_ref, 2, 1), (third_ref, up3_ref, 1, 2)):
        count = source.shape[2]
        order = lane_order(count, levels, copies)
        for k in range(0, K, 4):
            rows = source[k : k + 4].reshape(4 * K, count)
            target[k : k + 4] = dot(rows, order).astype(BF16).reshape(4, K, count * copies)


def prep_rest_kernel(up1_ref, up2_ref, up3_ref, c1_ref, c2_ref, c3_ref, d1_ref, d2_ref, d3_ref, m1_ref, m2_ref, m3_ref, ends_ref, wide_ref):
    for source, target in ((up1_ref, d1_ref), (up2_ref, d2_ref), (up3_ref, d3_ref)):
        for tile in range(source.shape[2] // LANES):
            lanes = slice(tile * LANES, (tile + 1) * LANES)
            wide_ref[...] = source[:, :, lanes].astype(F32).reshape(K * K, LANES)
            for m in range(K):
                target[m, :, lanes] = wide_ref[pl.ds(m, K, stride=K), :].astype(BF16)
    for source, target, levels, copies in ((c1_ref, m1_ref, 2, 1), (c2_ref, m2_ref, 1, 2)):
        count = source.shape[3]
        order = lane_order(count, levels, copies)
        for j in range(NC):
            for k in range(0, K, 8):
                rows = source[j, k : k + 8].reshape(8 * K, count)
                target[j, k : k + 8] = dot(rows, order).astype(BF16).reshape(8, K, LANES)
    low_ends = end_columns(LANES, 0)
    high_ends = end_columns(M, 4)
    for j in range(NC):
        for k in range(0, K, 8):
            low = dot(c1_ref[j, k : k + 8].reshape(8 * K, LANES), low_ends)
            high = dot(c2_ref[j, k : k + 8].reshape(8 * K, M), high_ends)
            ends_ref[j, k : k + 8] = (low + high).astype(BF16).reshape(8, K, LANES)
    top = c3_ref.shape[3]
    group = LANES // top
    for h in range(NFAR // group):
        for k in range(0, K, 8):
            total = None
            for q in range(group):
                put = jnp.where(iota((top, LANES), 0) + q * top == iota((top, LANES), 1), 1.0, 0.0).astype(BF16)
                part = dot(c3_ref[h * group + q, k : k + 8].reshape(8 * K, top), put)
                total = part if total is None else total + part
            m3_ref[h, k : k + 8] = total.astype(BF16).reshape(8, K, LANES)


def up_kernel(z_ref, basis_ref, up1_ref, up2_ref, up3_ref, sent_ref, coef1_ref, coef2_ref, rows_ref, x0_ref, x1_ref, x2_ref):
    rhs, order = z_ref.shape
    leaves = order // M
    top = leaves // 8
    low = iota((rhs, LANES), 1) < M
    zero = jnp.zeros((rhs, LANES), BF16)

    for outer in range(leaves // (4 * GROUPS)):
        coefs = []
        for inner in range(GROUPS):
            lanes = pl.ds(pl.multiple_of((outer * GROUPS + inner) * 256, 256), 256)
            z = z_ref[:, lanes]
            left, right = z[:, :LANES], z[:, LANES:]
            first = jnp.concatenate([jnp.where(low, left, zero), jnp.where(low, zero, left)], axis=0)
            second = jnp.concatenate([jnp.where(low, right, zero), jnp.where(low, zero, right)], axis=0)
            none = jnp.zeros_like(first)
            masked = jnp.concatenate(
                [jnp.concatenate([first, none], axis=1), jnp.concatenate([none, second], axis=1)], axis=0
            )
            coefs.append(lax.dot_general(masked, basis_ref[:, lanes], NT, preferred_element_type=F32))
        for inner in range(GROUPS):
            rows_ref[pl.ds(pl.multiple_of((outer * GROUPS + inner) * 64, 64), 64), :K] = coefs[inner]

    unit = jnp.where(iota((K, K), 0) == iota((K, K), 1), 1.0, 0.0).astype(BF16)
    for outer in range(rhs // 4):
        turned = []
        for inner in range(4):
            r = outer * 4 + inner
            pieces = []
            for c in range(2):
                for b in range(2):
                    for a in range(2):
                        pieces.append(rows_ref[pl.ds(rhs * (4 * a + 2 * b + c) + r, top, stride=8 * rhs), :K])
            tall = jnp.concatenate(pieces, axis=0).astype(BF16)
            turned.append(lax.dot_general(unit, tall, NT, preferred_element_type=F32))
        for inner in range(4):
            x0_ref[0, outer * 4 + inner] = turned[inner][:, :LANES]
            x0_ref[1, outer * 4 + inner] = turned[inner][:, LANES:]

    half = rhs // 2
    zeros = tuple(jnp.zeros((K, LANES), F32) for _ in range(half))
    for first in (0, half):
        terms = [
            (
                functools.partial(lambda s, k: up1_ref[k, :, s * LANES : (s + 1) * LANES], s),
                functools.partial(lambda s, r, k: x0_ref[s, first + r, pl.ds(k, 1), :], s),
            )
            for s in range(2)
        ]
        for r, acc in enumerate(contract(terms, zeros, LANES)):
            coef1_ref[first + r] = acc.astype(BF16)
            x1_ref[first + r] = rounded(acc)
    low = iota((K, LANES), 1) < M
    for first in (0, half):
        terms = [(lambda k: up2_ref[k], lambda r, k: x1_ref[first + r, pl.ds(k, 1), :])]
        for r, acc in enumerate(contract(terms, zeros, LANES)):
            total = rounded(acc + pltpu.roll(acc, 64, 1))
            if first == 0:
                x2_ref[r] = total
            else:
                both = jnp.where(low, x2_ref[r], total)
                x2_ref[r] = both
                coef2_ref[r] = both.astype(BF16)
    terms = [(lambda k: up3_ref[k], lambda r, k: x2_ref[r, pl.ds(k, 1), :])]
    sums = [acc + pltpu.roll(acc, 32, 1) for acc in contract(terms, zeros, LANES)]
    odd = (iota((K, LANES), 1) & 32) > 0
    for r in range(half // 2):
        sent_ref[r * K : (r + 1) * K] = jnp.where(odd, sums[r], pltpu.roll(sums[r + half // 2], 96, 1)).astype(BF16)

    def ends(count, offset, shift):
        row, column = iota((LANES, LANES), 0), iota((LANES, LANES), 1)
        hit = (row == -1)
        for copy in range(LANES // count):
            for e, node in enumerate((0, 1, count - 2, count - 1)):
                at = place_static(node, count, 2 if count == LANES else 1)
                hit = hit | ((row == copy * count + at) & (column == copy * M + offset + e))
        return jnp.where(hit, 1.0, 0.0).astype(BF16)

    first_ends = dot(x1_ref[...].astype(BF16).reshape(rhs * K, LANES), ends(LANES, 0, 0)).reshape(rhs, K, LANES)
    second_ends = dot(x2_ref[...].astype(BF16).reshape(half * K, LANES), ends(M, 4, 64)).reshape(half, K, LANES)
    packed = jnp.zeros((K, LANES), F32)
    for r in range(rhs):
        value = first_ends[r]
        if r < half:
            value = value + second_ends[r]
        packed = packed + (pltpu.roll(value, 8 * r, 1) if r else value)
    base = half // 2 * K
    sent_ref[base : base + K] = packed.astype(BF16)
    sent_ref[base + K : base + K + rhs] = z_ref[:, :LANES]
    sent_ref[base + K + rhs : base + K + 2 * rhs] = z_ref[:, order - LANES :]


def first_kernel(
    z_ref, basis_ref, first_ref, second_ref, third_ref,
    sent_ref, coef1_ref, coef2_ref, up1_ref, up2_ref, up3_ref, *scratch
):
    prep_up_kernel(first_ref, second_ref, third_ref, up1_ref, up2_ref, up3_ref)
    up_kernel(z_ref, basis_ref, up1_ref, up2_ref, up3_ref, sent_ref, coef1_ref, coef2_ref, *scratch)


def put_leaves(target_ref, tile, slot):
    low = iota(tile.shape, 1) < M
    wide = tile.astype(F32)
    swapped = pltpu.roll(wide, M, 1)
    target_ref[slot] = jnp.where(low, wide, swapped).astype(BF16)
    target_ref[slot + 1] = jnp.where(low, swapped, wide).astype(BF16)


def own_blocks(res, rhs):
    low = iota((rhs, LANES), 1) < M
    return jnp.concatenate(
        [
            jnp.where(low, res[:rhs, :LANES], res[rhs : 2 * rhs, :LANES]),
            jnp.where(low, res[2 * rhs : 3 * rhs, LANES:], res[3 * rhs :, LANES:]),
        ],
        axis=1,
    )


def near_group(read, weights, rhs):
    low = iota((rhs, LANES), 1) < M
    rows = []
    for leaf in range(4):
        z = [read(j, leaf) for j in range(NEAR)]
        rows.append(jnp.concatenate([jnp.where(low, z[0], z[1]), jnp.where(low, z[2], z[3]), z[4][:, :M]], axis=1))
    return own_blocks(dot(jnp.concatenate(rows, axis=0), weights), rhs)


def near_kernel(chunk0, leaves_ref, z_ref, blocks_ref, out_ref, z_leaves_ref):
    rhs, order = z_ref.shape
    chunks = out_ref.shape[1] // CHUNK
    per = CHUNK // M
    first_tile = max(chunk0 * (CHUNK // LANES) - 1, 0)
    last_tile = min((chunk0 + chunks) * (CHUNK // LANES) + 1, order // LANES)
    for t in range(first_tile, last_tile):
        put_leaves(z_leaves_ref, z_ref[:, t * LANES : (t + 1) * LANES], 2 * t + HN)

    @pl.loop(0, chunks)
    def _(c):
        for g in range(CHUNK // 256):
            leaf0 = (chunk0 + c) * per + 4 * g
            here = pl.ds(pl.multiple_of(c * CHUNK + g * 256, 256), 256)
            there = pl.ds(pl.multiple_of((chunk0 + c) * CHUNK + g * 256, 256), 256)
            weights = blocks_ref[:, :, there].reshape(NEAR * M, 256)
            out_ref[:, here] = near_group(lambda j, e: z_leaves_ref[leaves_ref[j, leaf0 + e]], weights, rhs)


def bit_reverse(value, bits):
    out = jnp.zeros_like(value)
    for b in range(bits):
        out = out + (((value >> b) & 1) << (bits - 1 - b))
    return out


def in_order(rows, count, levels):
    wide = jnp.concatenate([rows.astype(F32)] + [jnp.zeros((8 - rows.shape[0], count), F32)], axis=0).astype(BF16)
    return dot(wide, lane_order(count, levels)).astype(jnp.int32)


def own_rows_of(nodes, me, count, levels):
    local = nodes - me * count
    inside = (local >= 0) & (local < count)
    return in_order(jnp.where(inside, place(jnp.clip(local, 0, count - 1), count, levels), -1), count, levels)


def couple_kernel(me_ref, coef1_ref, coef2_ref, list1_ref, list2_ref, m1_ref, m2_ref, far1_ref, far2_ref, picks_ref):
    rhs, half = coef1_ref.shape[0], coef2_ref.shape[0]
    me = me_ref[0]
    zeros = tuple(jnp.zeros((K, LANES), F32) for _ in range(half))

    def run(matrix_ref, first):
        terms = [
            (
                functools.partial(lambda j, k: matrix_ref[j, k], j),
                functools.partial(lambda j, r, k: picks_ref[first + r, pl.ds(j * K + k, 1), :], j),
            )
            for j in range(NC)
        ]
        return contract(terms, zeros, LANES)

    rows = own_rows_of(list2_ref[...], me, M, 1)
    copy_of = iota((LANES, LANES), 1) // M
    tables = []
    for j in range(NC):
        row = jnp.concatenate([rows[j : j + 1], rows[j : j + 1]], axis=1)
        tables.append(jnp.where((iota((LANES, LANES), 0) - copy_of * M == row) & (row >= 0), 1.0, 0.0))
    table = jnp.concatenate(tables, axis=1).astype(BF16)
    picked = dot(coef2_ref[...].reshape(half * K, LANES), table).reshape(half, K, NC * LANES)
    for j in range(NC):
        picks_ref[:half, j * K : (j + 1) * K, :] = picked[:, :, j * LANES : (j + 1) * LANES]
    for r, acc in enumerate(run(m2_ref, 0)):
        far2_ref[r] = acc
    rows = own_rows_of(list1_ref[...], me, LANES, 2)
    table = jnp.concatenate(
        [jnp.where(iota((LANES, LANES), 0) == rows[j : j + 1], 1.0, 0.0) for j in range(NC)], axis=1
    ).astype(BF16)
    picked = dot(coef1_ref[...].reshape(rhs * K, LANES), table).reshape(rhs, K, NC * LANES)
    for j in range(NC):
        picks_ref[:, j * K : (j + 1) * K, :] = picked[:, :, j * LANES : (j + 1) * LANES]
    for first in (0, half):
        for r, acc in enumerate(run(m1_ref, first)):
            far1_ref[first + r] = acc


def halo_codes(nodes, me, count, offset):
    local = nodes - me * count
    code = jnp.where(local < 0, local + 5, jnp.where(local >= count, local - count + 1, 0))
    code = jnp.where(code > 0, code + offset, 0)
    wide = jnp.concatenate([code.astype(F32)] + [jnp.zeros((8 - code.shape[0], count), F32)], axis=0).astype(BF16)
    return dot(wide, end_columns(count, offset))


def down_kernel(bits, me_ref, leaves_ref, early_ref, late_ref, far1_in_ref, far2_in_ref, z_ref, *refs):
    near_refs = refs[:PIECES]
    (blocks_ref, basis_ref, list1_ref, list2_ref, top_ref, ends_ref, m3_ref, d1_ref, d2_ref, d3_ref,
     out_hbm, out_ref, every_ref, picks_ref, far1_ref, x_ref, x0_ref, rows_ref, z_leaves_ref, sems) = refs[PIECES:]
    rhs, order = z_ref.shape
    leaves = order // M
    top = leaves // 8
    half = rhs // 2
    me = me_ref[0]
    devices = 1 << bits
    own_rows = half // 2 * K

    def block(device, rows):
        at = bit_reverse(jnp.bitwise_xor(device, me), bits)
        early = early_ref[jnp.minimum(at, devices // 2 - 1), rows]
        late = late_ref[jnp.maximum(at - devices // 2, 0), rows]
        return jnp.where(at < devices // 2, early.astype(F32), late.astype(F32))

    before = jnp.maximum(me - 1, 0)
    after = jnp.minimum(me + 1, devices - 1)

    z_before = block(before, slice(own_rows + K + rhs, own_rows + K + 2 * rhs)).astype(BF16)
    z_after = block(after, slice(own_rows + K, own_rows + K + rhs)).astype(BF16)
    put_leaves(z_leaves_ref, z_before, 0)
    for t in range(3):
        put_leaves(z_leaves_ref, z_ref[:, t * LANES : (t + 1) * LANES], 2 + 2 * t)
        put_leaves(z_leaves_ref, z_ref[:, order - (3 - t) * LANES : order - (2 - t) * LANES or None], 8 + 2 * t)
    put_leaves(z_leaves_ref, z_after, 14)
    head = near_group(lambda j, e: z_leaves_ref[leaves_ref[j, e]], blocks_ref[:, :, :256].reshape(NEAR * M, 256), rhs)
    skip = leaves + 2 * HN - 16
    tail = near_group(
        lambda j, e: z_leaves_ref[leaves_ref[j, leaves - 4 + e] - skip], blocks_ref[:, :, order - 256 :].reshape(NEAR * M, 256), rhs
    )

    sides = slice(own_rows, own_rows + K)
    halo = jnp.where((iota((K, LANES), 1) & 2) > 0, block(before, sides), block(after, sides)).astype(BF16)
    codes = (halo_codes(list1_ref[...], me, LANES, 0) + halo_codes(list2_ref[...], me, M, 4)).astype(jnp.int32)
    lane_group = iota((LANES, LANES), 1) & -8
    sums = []
    for j in range(NC):
        code = codes[j : j + 1]
        table = jnp.where((iota((LANES, LANES), 0) == lane_group + code - 1) & (code > 0), 1.0, 0.0).astype(BF16)
        x_ref[j] = dot(halo, table)
    for j in range(NC):
        total = jnp.zeros((K, LANES), F32)
        for k in range(K):
            total = total + ends_ref[j, k].astype(F32) * x_ref[j, k : k + 1, :]
        sums.append(total)
    outer = sums[0] + sums[1] + sums[2]
    turned = jnp.concatenate([pltpu.roll(outer, LANES - 8 * r, 1) if r else outer for r in range(rhs)], axis=0)
    coarse = turned.astype(BF16)
    fine = (turned - coarse.astype(F32)).astype(BF16)

    def scatter(count, offset):
        row, column = iota((LANES, LANES), 0), iota((LANES, LANES), 1)
        hit = row < 0
        for copy in range(LANES // count):
            for e, node in enumerate(end_nodes(count)):
                at = place_static(node, count, 2 if count == LANES else 1)
                hit = hit | ((column == copy * count + at) & (row == copy * M + offset + e))
        return jnp.where(hit, 1.0, 0.0).astype(BF16)

    put = scatter(LANES, 0)
    outer1 = (dot(coarse, put) + dot(fine, put)).reshape(rhs, K, LANES)
    put = scatter(M, 4)
    outer2 = (dot(coarse[: half * K], put) + dot(fine[: half * K], put)).reshape(half, K, LANES)

    group = iota((own_rows, LANES), 1) // top
    per = LANES // top
    for tile in range(devices // per):
        source = early_ref if tile < devices // per // 2 else late_ref
        first = tile * per - (0 if tile < devices // per // 2 else devices // 2)
        parts = [source[first + q, :own_rows].astype(F32) for q in range(per)]
        for g in range(per):
            merged = None
            for q in range(per):
                shift = (q - g) * top % LANES
                moved = pltpu.roll(parts[q], shift, 1) if shift else parts[q]
                merged = moved if merged is None else jnp.where(group == q, moved, merged)
            every_ref[g * own_rows : (g + 1) * own_rows, tile * LANES : (tile + 1) * LANES] = merged.astype(BF16)
    nodes = top_ref[...]
    rows = bit_reverse(jnp.bitwise_xor(nodes // top, me), bits) * top + nodes % top
    hot = []
    for j in range(NFAR):
        hot.append(jnp.where(iota((devices * top, top), 0) == rows[j : j + 1], 1.0, 0.0).astype(BF16))
    for h in range(NFAR // per):
        wide = None
        for q in range(per):
            put = jnp.where(iota((top, LANES), 0) + q * top == iota((top, LANES), 1), 1.0, 0.0).astype(BF16)
            part = dot(hot[h * per + q], put)
            wide = part if wide is None else wide + part
        picked = dot(every_ref[...], wide.astype(BF16))
        picks_ref[:, h * K : (h + 1) * K, :] = picked.reshape(rhs, K, LANES)
    zeros = tuple(jnp.zeros((K, LANES), F32) for _ in range(half))
    groups_of = [1, 0, 3, 2]

    def slot(r):
        quarter = rhs // 4
        return groups_of[r // quarter] * quarter + r % quarter

    low = iota((K, LANES), 1) < M
    kept = {}
    for first in range(0, rhs, half):
        terms = [
            (
                functools.partial(lambda h, k: m3_ref[h, k], h),
                functools.partial(lambda h, r, k: picks_ref[slot(first + r), pl.ds(h * K + k, 1), :], h),
            )
            for h in range(NFAR // per)
        ]
        for r, acc in enumerate(contract(terms, zeros, LANES)):
            acc = acc + pltpu.roll(acc, 64, 1)
            acc = rounded(acc + pltpu.roll(acc, 32, 1))
            if first == 0:
                x_ref[r] = acc
            else:
                x_ref[r] = jnp.where(low, x_ref[r], acc)

    terms = [(lambda m: d3_ref[m], lambda r, m: x_ref[r, pl.ds(m, 1), :])]
    start = tuple(far2_in_ref[r] + outer2[r] for r in range(half))
    for r, acc in enumerate(contract(terms, start, LANES)):
        value = rounded(acc)
        swapped = pltpu.roll(value, M, 1)
        x_ref[r] = jnp.where(low, value, swapped)
        x_ref[r + half] = jnp.where(low, swapped, value)

    for first in (0, half):
        terms = [(lambda m: d2_ref[m], lambda r, m: x_ref[first + r, pl.ds(m, 1), :])]
        start = tuple(far1_in_ref[first + r] + outer1[first + r] for r in range(half))
        for r, acc in enumerate(contract(terms, start, LANES)):
            far1_ref[first + r] = rounded(acc)

    for first in (0, half):
        for s in range(2):
            lanes = slice(s * LANES, (s + 1) * LANES)
            terms = [(lambda m: d1_ref[m, :, lanes], lambda r, m: far1_ref[first + r, pl.ds(m, 1), :])]
            for r, acc in enumerate(contract(terms, zeros, LANES)):
                x0_ref[s, first + r] = acc
    unit = jnp.where(iota((leaves, leaves), 0) == iota((leaves, leaves), 1), 1.0, 0.0).astype(BF16)
    for outer in range(rhs // BATCH):
        turned = []
        for inner in range(BATCH):
            r = outer * BATCH + inner
            wide = jnp.concatenate([x0_ref[0, r], x0_ref[1, r]], axis=1).astype(BF16)
            turned.append(lax.dot_general(unit, wide, NT, preferred_element_type=F32))
        for inner in range(BATCH):
            at = 0
            for c in range(2):
                for b in range(2):
                    for a in range(2):
                        start = rhs * (4 * a + 2 * b + c) + outer * BATCH + inner
                        rows_ref[pl.ds(start, top, stride=8 * rhs), :K] = turned[inner][at : at + top]
                        at += top

    def far_group(g):
        lanes = slice(g * 256, (g + 1) * 256)
        coefs = rows_ref[g * 64 : (g + 1) * 64, :K].astype(BF16)
        return dot(coefs, basis_ref[:, lanes])

    total = leaves // 4
    parts = 4
    for part in range(parts):
        inside = range(part * total // parts, (part + 1) * total // parts)
        fars = [far_group(g) for g in inside]
        for g, far in zip(inside, fars):
            if g == 0:
                near = head
            elif g == total - 1:
                near = tail
            else:
                at = 0
                while g * 256 >= at + near_refs[0].shape[1]:
                    at += near_refs[0].shape[1]
                near = near_refs[at // near_refs[0].shape[1]][:, g * 256 - at : (g + 1) * 256 - at]
            out_ref[:, g * 256 : (g + 1) * 256] = (near + own_blocks(far, rhs)).astype(BF16)
        lanes = slice(part * order // parts, (part + 1) * order // parts)
        pltpu.make_async_copy(out_ref.at[:, lanes], out_hbm.at[:, lanes], sems.at[part]).start()
    for part in range(parts):
        lanes = slice(part * order // parts, (part + 1) * order // parts)
        pltpu.make_async_copy(out_ref.at[:, lanes], out_hbm.at[:, lanes], sems.at[part]).wait()


VM = pl.BlockSpec(memory_space=pltpu.VMEM)
SM = pl.BlockSpec(memory_space=pltpu.SMEM)
HBM = pl.BlockSpec(memory_space=pltpu.HBM)


def params(mib):
    return pltpu.CompilerParams(vmem_limit_bytes=mib * 2**20)


def cost(flops, moved):
    return pl.CostEstimate(flops=flops, bytes_accessed=moved, transcendentals=0)


def shape(dims, kind=BF16):
    return jax.ShapeDtypeStruct(dims, kind)


def body(
    right_sides, near_blocks, near_leaves, leaf_basis, transfer_first, transfer_second, transfer_third,
    coupling_first, coupling_second, list_first, list_second, top_coupling, top_nodes,
):
    position = lax.axis_index(AXES)
    devices = lax.axis_size("branch") * lax.axis_size("sub")
    bits = devices.bit_length() - 1
    rhs, order = right_sides.shape
    leaves = order // M
    half = rhs // 2
    me = position.astype(jnp.int32).reshape(1)
    near_local = near_leaves.T - (position * leaves - HN)
    lists = (list_first.T, list_second.T, top_nodes.T)

    sent_rows = half // 2 * K + K + 2 * rhs
    up_shapes = (shape((sent_rows, LANES)), shape((rhs, K, LANES)), shape((half, K, LANES)))
    up_scratch = [
        pltpu.VMEM((leaves * rhs, LANES), F32),
        pltpu.VMEM((leaves // LANES, rhs, K, LANES), F32),
        pltpu.VMEM((rhs, K, LANES), F32),
        pltpu.VMEM((half, K, LANES), F32),
    ]
    *upward, up1, up2, up3 = pl.pallas_call(
        first_kernel,
        out_shape=up_shapes
        + (shape((K, K, leaves)), shape((K, K, LANES)), shape((K, K, LANES))),
        in_specs=[VM] * 5,
        out_specs=(VM,) * 6,
        scratch_shapes=up_scratch,
        compiler_params=params(12),
        cost_estimate=cost(FIRST * 10**9, 3 * 2**20),
    )(right_sides, leaf_basis, transfer_first, transfer_second, transfer_third)
    vectors, basis, blocks = right_sides, leaf_basis, near_blocks
    cut = order // PIECES

    def prepare(up1, up2, up3):
        return pl.pallas_call(
            prep_rest_kernel,
            out_shape=(
                shape((K, K, leaves)), shape((K, K, LANES)), shape((K, K, LANES)),
                shape((NC, K, K, LANES)), shape((NC, K, K, LANES)),
                shape((NFAR * top_coupling.shape[3] // LANES, K, K, LANES)), shape((NC, K, K, LANES)),
            ),
            in_specs=[VM] * 6,
            out_specs=(VM,) * 7,
            scratch_shapes=[pltpu.VMEM((K * K, LANES), F32)],
            compiler_params=params(16),
            cost_estimate=cost(10**9, 9 * 2**20),
        )(up1, up2, up3, coupling_first, coupling_second, top_coupling)

    def near_piece(i, vectors):
        return pl.pallas_call(
            functools.partial(near_kernel, i * cut // CHUNK),
            out_shape=shape((rhs, cut), F32),
            in_specs=[SM, VM, VM],
            out_specs=VM,
            scratch_shapes=[pltpu.VMEM((leaves + 2 * HN, rhs, LANES), BF16)],
            compiler_params=params(16),
            cost_estimate=cost(10**9, 8 * 2**20),
        )(near_local, vectors, blocks)

    def couple(coef1, coef2, m1, m2):
        return pl.pallas_call(
            couple_kernel,
            out_shape=(shape((rhs, K, LANES), F32), shape((half, K, LANES), F32)),
            in_specs=[SM] + [VM] * 6,
            out_specs=(VM,) * 2,
            scratch_shapes=[pltpu.VMEM((rhs, NC * K, LANES), F32)],
            compiler_params=params(16),
            cost_estimate=cost(10**9, 8 * 2**20),
        )(me, coef1, coef2, lists[0], lists[1], m1, m2)

    def exchange(sent, works):
        every, done = sent[None], []
        for step, b in enumerate(reversed(range(bits))):
            pairs = [(i, i ^ (1 << b)) for i in range(devices)]
            other = lax.ppermute(every, AXES, pairs)
            if step < len(works):
                result = works[step](every)
                other, result = lax.optimization_barrier((other, result))
                done.append(result)
            if b:
                every = jnp.concatenate([every, other], axis=0)
        return every, other, done

    def held(values, every):
        return lax.optimization_barrier((*values, every))[:-1]

    def down(every, other, far1, far2, vectors, nears, prepared, keep):
        d1, d2, d3, _, _, m3, ends = prepared
        out = shape((rhs, order))
        results = pl.pallas_call(
            functools.partial(down_kernel, bits),
            out_shape=(out, out) if keep else (out,),
            in_specs=[SM, SM] + [VM] * 5 + [VM] * PIECES + [VM] * 10,
            out_specs=(HBM, VM) if keep else (HBM,),
            scratch_shapes=([] if keep else [pltpu.VMEM((rhs, order), BF16)])
            + [
                pltpu.VMEM((rhs * K, devices * (leaves // 8)), BF16),
                pltpu.VMEM((rhs, NFAR * K * (leaves // 8) // LANES, LANES), F32),
                pltpu.VMEM((rhs, K, LANES), F32),
                pltpu.VMEM((rhs, K, LANES), F32),
                pltpu.VMEM((leaves // LANES, rhs, K, LANES), F32),
                pltpu.VMEM((leaves * rhs, LANES), F32),
                pltpu.VMEM((16, rhs, LANES), BF16),
                pltpu.SemaphoreType.DMA((4,)),
            ],
            compiler_params=params(24),
            cost_estimate=cost(10**9, 8 * 2**20),
        )(me, near_local, every, other, far1, far2, vectors, *nears, blocks, basis, *lists, ends, m3, d1, d2, d3)
        return results

    sent, coef1, coef2 = upward
    prepared = []
    works = [
        lambda every: near_piece(0, *held((vectors,), every)),
        lambda every: prepared.extend(prepare(*held((up1, up2, up3), every))) or tuple(prepared),
        lambda every: couple(*held((coef1, coef2), every), *prepared[3:5]),
        lambda every: near_piece(1, *held((vectors,), every)),
    ]
    every, other, (near0, prepared, fars, near1) = exchange(sent, works)
    first_image, second_vectors = down(every, other, *fars, vectors, (near0, near1), prepared, True)
    sent, coef1, coef2 = pl.pallas_call(
        up_kernel,
        out_shape=up_shapes,
        in_specs=[VM] * 5,
        out_specs=(VM,) * 3,
        scratch_shapes=up_scratch,
        compiler_params=params(12),
        cost_estimate=cost(10**8, 3 * 2**20),
    )(second_vectors, basis, up1, up2, up3)
    works = [
        lambda every: near_piece(0, *held((second_vectors,), every)),
        lambda every: near_piece(1, *held((second_vectors,), every)),
        lambda every: couple(*held((coef1, coef2), every), *prepared[3:5]),
    ]
    every, other, (near0, near1, fars) = exchange(sent, works)
    (second_image,) = down(every, other, *fars, second_vectors, (near0, near1), prepared, False)
    return (first_image, second_image)


def solution(mesh):
    tree = P(None, None, AXES)
    placed = (
        P("groups", AXES), tree, P(AXES, None), P(None, AXES), tree, tree, tree,
        P(None, None, None, AXES), P(None, None, None, AXES), P(AXES, None), P(AXES, None),
        P(None, None, None, AXES), P(AXES, None),
    )
    return jax.shard_map(
        body, mesh=mesh, in_specs=placed, out_specs=(P("groups", AXES), P("groups", AXES)), check_vma=False
    )
```

```python
import functools

import jax
import jax.numpy as jnp
from jax import lax
from jax.experimental import pallas as pl
from jax.experimental.pallas import tpu as pltpu
from jax.sharding import PartitionSpec as P

M = 64
K = 32
NEAR = 5
NC = 3
NFAR = 8
HN = 2
HC = 2
LANES = 128
AXES = ("branch", "sub")
PIECES = 2
UNROLL = 32
FIRST = 1
CHUNK = 1024
F32 = jnp.float32
BF16 = jnp.bfloat16
NT = (((1,), (1,)), ((), ()))


def iota(shape, dim):
    return lax.broadcasted_iota(jnp.int32, shape, dim)


def place(node, count, levels):
    where = jnp.zeros_like(node)
    for level in range(levels):
        count //= 2
        where = where + (node & 1) * count
        node = node >> 1
    return where + node


def place_static(node, count, levels):
    where = 0
    for level in range(levels):
        count //= 2
        where += (node & 1) * count
        node >>= 1
    return where + node


def lane_order(count, levels, copies=1):
    rows = place(iota((count, count * copies), 0), count, levels)
    columns = iota((count, count * copies), 1) & (count - 1)
    return jnp.where(rows == columns, 1.0, 0.0).astype(BF16)


def dot(a, b):
    return jnp.dot(a, b, preferred_element_type=F32)


def end_nodes(count):
    return (0, 1, count - 2, count - 1)


def end_columns(count, offset):
    row, lane = iota((count, LANES), 0), iota((count, LANES), 1) & 7
    hit = row < 0
    for e, node in enumerate(end_nodes(count)):
        hit = hit | ((row == node) & (lane == offset + e))
    return jnp.where(hit, 1.0, 0.0).astype(BF16)


def rounded(x):
    return x.astype(BF16).astype(F32)


def contract(terms, init, lanes):
    def step(position, accs):
        for matrix_at, x_at in terms:
            matrix = matrix_at(position).astype(F32)
            accs = tuple(acc + matrix * x_at(r, position) for r, acc in enumerate(accs))
        return accs

    return lax.fori_loop(0, K, step, init, unroll=UNROLL)


def prep_up_kernel(first_ref, second_ref, third_ref, up1_ref, up2_ref, up3_ref):
    for source, target, levels, copies in ((first_ref, up1_ref, 3, 1), (second_ref, up2_ref, 2, 1), (third_ref, up3_ref, 1, 2)):
        count = source.shape[2]
        order = lane_order(count, levels, copies)
        for k in range(0, K, 4):
            rows = source[k : k + 4].reshape(4 * K, count)
            target[k : k + 4] = dot(rows, order).astype(BF16).reshape(4, K, count * copies)


def prep_rest_kernel(up1_ref, up2_ref, up3_ref, c1_ref, c2_ref, c3_ref, d1_ref, d2_ref, d3_ref, m1_ref, m2_ref, m3_ref, ends_ref, wide_ref):
    for source, target in ((up1_ref, d1_ref), (up2_ref, d2_ref), (up3_ref, d3_ref)):
        for tile in range(source.shape[2] // LANES):
            lanes = slice(tile * LANES, (tile + 1) * LANES)
            wide_ref[...] = source[:, :, lanes].astype(F32).reshape(K * K, LANES)
            for m in range(K):
                target[m, :, lanes] = wide_ref[pl.ds(m, K, stride=K), :].astype(BF16)
    for source, target, levels, copies in ((c1_ref, m1_ref, 2, 1), (c2_ref, m2_ref, 1, 2)):
        count = source.shape[3]
        order = lane_order(count, levels, copies)
        for j in range(NC):
            for k in range(0, K, 8):
                rows = source[j, k : k + 8].reshape(8 * K, count)
                target[j, k : k + 8] = dot(rows, order).astype(BF16).reshape(8, K, LANES)
    low_ends = end_columns(LANES, 0)
    high_ends = end_columns(M, 4)
    for j in range(NC):
        for k in range(0, K, 8):
            low = dot(c1_ref[j, k : k + 8].reshape(8 * K, LANES), low_ends)
            high = dot(c2_ref[j, k : k + 8].reshape(8 * K, M), high_ends)
            ends_ref[j, k : k + 8] = (low + high).astype(BF16).reshape(8, K, LANES)
    top = c3_ref.shape[3]
    group = LANES // top
    for h in range(NFAR // group):
        for k in range(0, K, 8):
            total = None
            for q in range(group):
                put = jnp.where(iota((top, LANES), 0) + q * top == iota((top, LANES), 1), 1.0, 0.0).astype(BF16)
                part = dot(c3_ref[h * group + q, k : k + 8].reshape(8 * K, top), put)
                total = part if total is None else total + part
            m3_ref[h, k : k + 8] = total.astype(BF16).reshape(8, K, LANES)


def spread_basis(part):
    low = iota((K, LANES), 1) < M
    zero = jnp.zeros((K, LANES), BF16)
    left, right = part[:, :LANES], part[:, LANES:]
    first = jnp.concatenate([jnp.where(low, left, zero), jnp.where(low, zero, left), zero, zero], axis=0)
    second = jnp.concatenate([zero, zero, jnp.where(low, right, zero), jnp.where(low, zero, right)], axis=0)
    return jnp.concatenate([first, second], axis=1)


def up_kernel(z_ref, basis_ref, up1_ref, up2_ref, up3_ref, sent_ref, coef1_ref, coef2_ref, rows_ref, x0_ref, x1_ref, x2_ref):
    rhs, order = z_ref.shape
    leaves = order // M
    top = leaves // 8
    groups = leaves // 4
    for g in range(groups):
        lanes = slice(g * 256, (g + 1) * 256)
        rows_ref[g * rhs : (g + 1) * rhs] = lax.dot_general(
            z_ref[:, lanes], spread_basis(basis_ref[:, lanes]), NT, preferred_element_type=F32
        )
    unit = jnp.where(iota((LANES, LANES), 0) == iota((LANES, LANES), 1), 1.0, 0.0).astype(BF16)
    for r in range(rhs):
        pieces = [rows_ref[pl.ds(a * rhs + r, top, stride=2 * rhs), :] for a in range(2)]
        flat = jnp.concatenate(pieces, axis=0).astype(BF16)
        both = jnp.concatenate([flat, flat], axis=0)
        tall = lax.dot_general(unit, both, NT, preferred_element_type=F32)
        keep = iota((K, LANES), 1) < M
        for c in range(2):
            x0_ref[c, r] = jnp.where(keep, tall[c * K : (c + 1) * K], tall[(2 + c) * K : (3 + c) * K])

    half = rhs // 2
    zeros = tuple(jnp.zeros((K, LANES), F32) for _ in range(half))
    for first in (0, half):
        terms = [
            (
                functools.partial(lambda s, k: up1_ref[k, :, s * LANES : (s + 1) * LANES], s),
                functools.partial(lambda s, r, k: x0_ref[s, first + r, pl.ds(k, 1), :], s),
            )
            for s in range(2)
        ]
        for r, acc in enumerate(contract(terms, zeros, LANES)):
            coef1_ref[first + r] = acc.astype(BF16)
            x1_ref[first + r] = rounded(acc)
    low = iota((K, LANES), 1) < M
    for first in (0, half):
        terms = [(lambda k: up2_ref[k], lambda r, k: x1_ref[first + r, pl.ds(k, 1), :])]
        for r, acc in enumerate(contract(terms, zeros, LANES)):
            total = rounded(acc + pltpu.roll(acc, 64, 1))
            if first == 0:
                x2_ref[r] = total
            else:
                both = jnp.where(low, x2_ref[r], total)
                x2_ref[r] = both
                coef2_ref[r] = both.astype(BF16)
    terms = [(lambda k: up3_ref[k], lambda r, k: x2_ref[r, pl.ds(k, 1), :])]
    sums = [acc + pltpu.roll(acc, 32, 1) for acc in contract(terms, zeros, LANES)]
    odd = (iota((K, LANES), 1) & 32) > 0
    for r in range(half // 2):
        sent_ref[r * K : (r + 1) * K] = jnp.where(odd, sums[r], pltpu.roll(sums[r + half // 2], 96, 1)).astype(BF16)

    def ends(count, offset, shift):
        row, column = iota((LANES, LANES), 0), iota((LANES, LANES), 1)
        hit = (row == -1)
        for copy in range(LANES // count):
            for e, node in enumerate((0, 1, count - 2, count - 1)):
                at = place_static(node, count, 2 if count == LANES else 1)
                hit = hit | ((row == copy * count + at) & (column == copy * M + offset + e))
        return jnp.where(hit, 1.0, 0.0).astype(BF16)

    first_ends = dot(x1_ref[...].astype(BF16).reshape(rhs * K, LANES), ends(LANES, 0, 0)).reshape(rhs, K, LANES)
    second_ends = dot(x2_ref[...].astype(BF16).reshape(half * K, LANES), ends(M, 4, 64)).reshape(half, K, LANES)
    packed = jnp.zeros((K, LANES), F32)
    for r in range(rhs):
        value = first_ends[r]
        if r < half:
            value = value + second_ends[r]
        packed = packed + (pltpu.roll(value, 8 * r, 1) if r else value)
    base = half // 2 * K
    sent_ref[base : base + K] = packed.astype(BF16)
    sent_ref[base + K : base + K + rhs] = z_ref[:, :LANES]
    sent_ref[base + K + rhs : base + K + 2 * rhs] = z_ref[:, order - LANES :]


def first_kernel(
    z_ref, basis_ref, first_ref, second_ref, third_ref,
    sent_ref, coef1_ref, coef2_ref, up1_ref, up2_ref, up3_ref, *scratch
):
    prep_up_kernel(first_ref, second_ref, third_ref, up1_ref, up2_ref, up3_ref)
    up_kernel(z_ref, basis_ref, up1_ref, up2_ref, up3_ref, sent_ref, coef1_ref, coef2_ref, *scratch)


def put_leaves(target_ref, tile, slot):
    low = iota(tile.shape, 1) < M
    wide = tile.astype(F32)
    swapped = pltpu.roll(wide, M, 1)
    target_ref[slot] = jnp.where(low, wide, swapped).astype(BF16)
    target_ref[slot + 1] = jnp.where(low, swapped, wide).astype(BF16)


def own_blocks(res, rhs):
    low = iota((rhs, LANES), 1) < M
    return jnp.concatenate(
        [
            jnp.where(low, res[:rhs, :LANES], res[rhs : 2 * rhs, :LANES]),
            jnp.where(low, res[2 * rhs : 3 * rhs, LANES:], res[3 * rhs :, LANES:]),
        ],
        axis=1,
    )


def near_group(read, weights, rhs):
    low = iota((rhs, LANES), 1) < M
    rows = []
    for leaf in range(4):
        z = [read(j, leaf) for j in range(NEAR)]
        rows.append(jnp.concatenate([jnp.where(low, z[0], z[1]), jnp.where(low, z[2], z[3]), z[4][:, :M]], axis=1))
    return own_blocks(dot(jnp.concatenate(rows, axis=0), weights), rhs)


def near_kernel(chunk0, leaves_ref, z_ref, blocks_ref, out_ref, z_leaves_ref):
    rhs, order = z_ref.shape
    chunks = out_ref.shape[1] // CHUNK
    per = CHUNK // M
    first_tile = max(chunk0 * (CHUNK // LANES) - 1, 0)
    last_tile = min((chunk0 + chunks) * (CHUNK // LANES) + 1, order // LANES)
    for t in range(first_tile, last_tile):
        put_leaves(z_leaves_ref, z_ref[:, t * LANES : (t + 1) * LANES], 2 * t + HN)

    @pl.loop(0, chunks)
    def _(c):
        for g in range(CHUNK // 256):
            leaf0 = (chunk0 + c) * per + 4 * g
            here = pl.ds(pl.multiple_of(c * CHUNK + g * 256, 256), 256)
            there = pl.ds(pl.multiple_of((chunk0 + c) * CHUNK + g * 256, 256), 256)
            weights = blocks_ref[:, :, there].reshape(NEAR * M, 256)
            out_ref[:, here] = near_group(lambda j, e: z_leaves_ref[leaves_ref[j, leaf0 + e]], weights, rhs)


def bit_reverse(value, bits):
    out = jnp.zeros_like(value)
    for b in range(bits):
        out = out + (((value >> b) & 1) << (bits - 1 - b))
    return out


def in_order(rows, count, levels):
    wide = jnp.concatenate([rows.astype(F32)] + [jnp.zeros((8 - rows.shape[0], count), F32)], axis=0).astype(BF16)
    return dot(wide, lane_order(count, levels)).astype(jnp.int32)


def own_rows_of(nodes, me, count, levels):
    local = nodes - me * count
    inside = (local >= 0) & (local < count)
    return in_order(jnp.where(inside, place(jnp.clip(local, 0, count - 1), count, levels), -1), count, levels)


def couple_kernel(me_ref, coef1_ref, coef2_ref, list1_ref, list2_ref, m1_ref, m2_ref, far1_ref, far2_ref, picks_ref):
    rhs, half = coef1_ref.shape[0], coef2_ref.shape[0]
    me = me_ref[0]
    zeros = tuple(jnp.zeros((K, LANES), F32) for _ in range(half))

    def run(matrix_ref, first):
        terms = [
            (
                functools.partial(lambda j, k: matrix_ref[j, k], j),
                functools.partial(lambda j, r, k: picks_ref[first + r, pl.ds(j * K + k, 1), :], j),
            )
            for j in range(NC)
        ]
        return contract(terms, zeros, LANES)

    rows = own_rows_of(list2_ref[...], me, M, 1)
    copy_of = iota((LANES, LANES), 1) // M
    tables = []
    for j in range(NC):
        row = jnp.concatenate([rows[j : j + 1], rows[j : j + 1]], axis=1)
        tables.append(jnp.where((iota((LANES, LANES), 0) - copy_of * M == row) & (row >= 0), 1.0, 0.0))
    table = jnp.concatenate(tables, axis=1).astype(BF16)
    picked = dot(coef2_ref[...].reshape(half * K, LANES), table).reshape(half, K, NC * LANES)
    for j in range(NC):
        picks_ref[:half, j * K : (j + 1) * K, :] = picked[:, :, j * LANES : (j + 1) * LANES]
    for r, acc in enumerate(run(m2_ref, 0)):
        far2_ref[r] = acc
    rows = own_rows_of(list1_ref[...], me, LANES, 2)
    table = jnp.concatenate(
        [jnp.where(iota((LANES, LANES), 0) == rows[j : j + 1], 1.0, 0.0) for j in range(NC)], axis=1
    ).astype(BF16)
    picked = dot(coef1_ref[...].reshape(rhs * K, LANES), table).reshape(rhs, K, NC * LANES)
    for j in range(NC):
        picks_ref[:, j * K : (j + 1) * K, :] = picked[:, :, j * LANES : (j + 1) * LANES]
    for first in (0, half):
        for r, acc in enumerate(run(m1_ref, first)):
            far1_ref[first + r] = acc


def halo_codes(nodes, me, count, offset):
    local = nodes - me * count
    code = jnp.where(local < 0, local + 5, jnp.where(local >= count, local - count + 1, 0))
    code = jnp.where(code > 0, code + offset, 0)
    wide = jnp.concatenate([code.astype(F32)] + [jnp.zeros((8 - code.shape[0], count), F32)], axis=0).astype(BF16)
    return dot(wide, end_columns(count, offset))


def down_kernel(bits, me_ref, leaves_ref, early_ref, late_ref, far1_in_ref, far2_in_ref, z_ref, *refs):
    near_refs = refs[:PIECES]
    (blocks_ref, basis_ref, list1_ref, list2_ref, top_ref, ends_ref, m3_ref, d1_ref, d2_ref, d3_ref,
     out_hbm, out_ref, every_ref, picks_ref, far1_ref, x_ref, x0_ref, rows_ref, z_leaves_ref, sems) = refs[PIECES:]
    rhs, order = z_ref.shape
    leaves = order // M
    top = leaves // 8
    half = rhs // 2
    me = me_ref[0]
    devices = 1 << bits
    own_rows = half // 2 * K

    def block(device, rows):
        at = bit_reverse(jnp.bitwise_xor(device, me), bits)
        early = early_ref[jnp.minimum(at, devices // 2 - 1), rows]
        late = late_ref[jnp.maximum(at - devices // 2, 0), rows]
        return jnp.where(at < devices // 2, early.astype(F32), late.astype(F32))

    before = jnp.maximum(me - 1, 0)
    after = jnp.minimum(me + 1, devices - 1)

    z_before = block(before, slice(own_rows + K + rhs, own_rows + K + 2 * rhs)).astype(BF16)
    z_after = block(after, slice(own_rows + K, own_rows + K + rhs)).astype(BF16)
    put_leaves(z_leaves_ref, z_before, 0)
    for t in range(3):
        put_leaves(z_leaves_ref, z_ref[:, t * LANES : (t + 1) * LANES], 2 + 2 * t)
        put_leaves(z_leaves_ref, z_ref[:, order - (3 - t) * LANES : order - (2 - t) * LANES or None], 8 + 2 * t)
    put_leaves(z_leaves_ref, z_after, 14)
    head = near_group(lambda j, e: z_leaves_ref[leaves_ref[j, e]], blocks_ref[:, :, :256].reshape(NEAR * M, 256), rhs)
    skip = leaves + 2 * HN - 16
    tail = near_group(
        lambda j, e: z_leaves_ref[leaves_ref[j, leaves - 4 + e] - skip], blocks_ref[:, :, order - 256 :].reshape(NEAR * M, 256), rhs
    )

    sides = slice(own_rows, own_rows + K)
    halo = jnp.where((iota((K, LANES), 1) & 2) > 0, block(before, sides), block(after, sides)).astype(BF16)
    codes = (halo_codes(list1_ref[...], me, LANES, 0) + halo_codes(list2_ref[...], me, M, 4)).astype(jnp.int32)
    lane_group = iota((LANES, LANES), 1) & -8
    sums = []
    for j in range(NC):
        code = codes[j : j + 1]
        table = jnp.where((iota((LANES, LANES), 0) == lane_group + code - 1) & (code > 0), 1.0, 0.0).astype(BF16)
        x_ref[j] = dot(halo, table)
    for j in range(NC):
        total = jnp.zeros((K, LANES), F32)
        for k in range(K):
            total = total + ends_ref[j, k].astype(F32) * x_ref[j, k : k + 1, :]
        sums.append(total)
    outer = sums[0] + sums[1] + sums[2]
    turned = jnp.concatenate([pltpu.roll(outer, LANES - 8 * r, 1) if r else outer for r in range(rhs)], axis=0)
    coarse = turned.astype(BF16)
    fine = (turned - coarse.astype(F32)).astype(BF16)

    def scatter(count, offset):
        row, column = iota((LANES, LANES), 0), iota((LANES, LANES), 1)
        hit = row < 0
        for copy in range(LANES // count):
            for e, node in enumerate(end_nodes(count)):
                at = place_static(node, count, 2 if count == LANES else 1)
                hit = hit | ((column == copy * count + at) & (row == copy * M + offset + e))
        return jnp.where(hit, 1.0, 0.0).astype(BF16)

    put = scatter(LANES, 0)
    outer1 = (dot(coarse, put) + dot(fine, put)).reshape(rhs, K, LANES)
    put = scatter(M, 4)
    outer2 = (dot(coarse[: half * K], put) + dot(fine[: half * K], put)).reshape(half, K, LANES)

    group = iota((own_rows, LANES), 1) // top
    per = LANES // top
    for tile in range(devices // per):
        source = early_ref if tile < devices // per // 2 else late_ref
        first = tile * per - (0 if tile < devices // per // 2 else devices // 2)
        parts = [source[first + q, :own_rows].astype(F32) for q in range(per)]
        for g in range(per):
            merged = None
            for q in range(per):
                shift = (q - g) * top % LANES
                moved = pltpu.roll(parts[q], shift, 1) if shift else parts[q]
                merged = moved if merged is None else jnp.where(group == q, moved, merged)
            every_ref[g * own_rows : (g + 1) * own_rows, tile * LANES : (tile + 1) * LANES] = merged.astype(BF16)
    nodes = top_ref[...]
    rows = bit_reverse(jnp.bitwise_xor(nodes // top, me), bits) * top + nodes % top
    hot = []
    for j in range(NFAR):
        hot.append(jnp.where(iota((devices * top, top), 0) == rows[j : j + 1], 1.0, 0.0).astype(BF16))
    for h in range(NFAR // per):
        wide = None
        for q in range(per):
            put = jnp.where(iota((top, LANES), 0) + q * top == iota((top, LANES), 1), 1.0, 0.0).astype(BF16)
            part = dot(hot[h * per + q], put)
            wide = part if wide is None else wide + part
        picked = dot(every_ref[...], wide.astype(BF16))
        picks_ref[:, h * K : (h + 1) * K, :] = picked.reshape(rhs, K, LANES)
    zeros = tuple(jnp.zeros((K, LANES), F32) for _ in range(half))
    groups_of = [1, 0, 3, 2]

    def slot(r):
        quarter = rhs // 4
        return groups_of[r // quarter] * quarter + r % quarter

    low = iota((K, LANES), 1) < M
    kept = {}
    for first in range(0, rhs, half):
        terms = [
            (
                functools.partial(lambda h, k: m3_ref[h, k], h),
                functools.partial(lambda h, r, k: picks_ref[slot(first + r), pl.ds(h * K + k, 1), :], h),
            )
            for h in range(NFAR // per)
        ]
        for r, acc in enumerate(contract(terms, zeros, LANES)):
            acc = acc + pltpu.roll(acc, 64, 1)
            acc = rounded(acc + pltpu.roll(acc, 32, 1))
            if first == 0:
                x_ref[r] = acc
            else:
                x_ref[r] = jnp.where(low, x_ref[r], acc)

    terms = [(lambda m: d3_ref[m], lambda r, m: x_ref[r, pl.ds(m, 1), :])]
    start = tuple(far2_in_ref[r] + outer2[r] for r in range(half))
    for r, acc in enumerate(contract(terms, start, LANES)):
        value = rounded(acc)
        swapped = pltpu.roll(value, M, 1)
        x_ref[r] = jnp.where(low, value, swapped)
        x_ref[r + half] = jnp.where(low, swapped, value)

    for first in (0, half):
        terms = [(lambda m: d2_ref[m], lambda r, m: x_ref[first + r, pl.ds(m, 1), :])]
        start = tuple(far1_in_ref[first + r] + outer1[first + r] for r in range(half))
        for r, acc in enumerate(contract(terms, start, LANES)):
            far1_ref[first + r] = rounded(acc)

    for first in (0, half):
        for s in range(2):
            lanes = slice(s * LANES, (s + 1) * LANES)
            terms = [(lambda m: d1_ref[m, :, lanes], lambda r, m: far1_ref[first + r, pl.ds(m, 1), :])]
            for r, acc in enumerate(contract(terms, zeros, LANES)):
                x0_ref[s, first + r] = acc
    groups = leaves // 4
    node = iota((LANES, LANES), 0) & (groups - 1)
    lane = (iota((LANES, LANES), 0) & -groups) + (node & 1) * top + (node >> 1)
    turn = jnp.where(lane == iota((LANES, LANES), 1), 1.0, 0.0).astype(BF16)
    for r in range(rhs):
        flat = jnp.concatenate([x0_ref[0, r], x0_ref[1, r]], axis=0).astype(BF16)
        both = jnp.concatenate([flat, flat], axis=0)
        tall = lax.dot_general(turn, both, NT, preferred_element_type=F32)
        keep = iota((groups, LANES), 1) < M
        rows_ref[pl.ds(r, groups, stride=rhs), :] = jnp.where(keep, tall[:groups], tall[groups:])

    def far_group(g):
        lanes = slice(g * 256, (g + 1) * 256)
        coefs = rows_ref[g * rhs : (g + 1) * rhs].astype(BF16)
        return dot(coefs, spread_basis(basis_ref[:, lanes]))

    total = leaves // 4
    parts = 4
    for part in range(parts):
        inside = range(part * total // parts, (part + 1) * total // parts)
        fars = [far_group(g) for g in inside]
        for g, far in zip(inside, fars):
            if g == 0:
                near = head
            elif g == total - 1:
                near = tail
            else:
                at = 0
                while g * 256 >= at + near_refs[0].shape[1]:
                    at += near_refs[0].shape[1]
                near = near_refs[at // near_refs[0].shape[1]][:, g * 256 - at : (g + 1) * 256 - at]
            out_ref[:, g * 256 : (g + 1) * 256] = (near + far).astype(BF16)
        lanes = slice(part * order // parts, (part + 1) * order // parts)
        pltpu.make_async_copy(out_ref.at[:, lanes], out_hbm.at[:, lanes], sems.at[part]).start()
    for part in range(parts):
        lanes = slice(part * order // parts, (part + 1) * order // parts)
        pltpu.make_async_copy(out_ref.at[:, lanes], out_hbm.at[:, lanes], sems.at[part]).wait()


VM = pl.BlockSpec(memory_space=pltpu.VMEM)
SM = pl.BlockSpec(memory_space=pltpu.SMEM)
HBM = pl.BlockSpec(memory_space=pltpu.HBM)


def params(mib):
    return pltpu.CompilerParams(vmem_limit_bytes=mib * 2**20)


def whole(array):
    return pl.BlockSpec(array.shape, lambda i: (0,) * len(array.shape), pipeline_mode=pl.Buffered(1))


def cost(flops, moved):
    return pl.CostEstimate(flops=flops, bytes_accessed=moved, transcendentals=0)


def shape(dims, kind=BF16):
    return jax.ShapeDtypeStruct(dims, kind)


def body(
    right_sides, near_blocks, near_leaves, leaf_basis, transfer_first, transfer_second, transfer_third,
    coupling_first, coupling_second, list_first, list_second, top_coupling, top_nodes,
):
    position = lax.axis_index(AXES)
    devices = lax.axis_size("branch") * lax.axis_size("sub")
    bits = devices.bit_length() - 1
    rhs, order = right_sides.shape
    leaves = order // M
    half = rhs // 2
    me = position.astype(jnp.int32).reshape(1)
    near_local = near_leaves.T - (position * leaves - HN)
    lists = (list_first.T, list_second.T, top_nodes.T)

    sent_rows = half // 2 * K + K + 2 * rhs
    up_shapes = (shape((sent_rows, LANES)), shape((rhs, K, LANES)), shape((half, K, LANES)))
    up_scratch = [
        pltpu.VMEM((leaves // 4 * rhs, LANES), F32),
        pltpu.VMEM((leaves // LANES, rhs, K, LANES), F32),
        pltpu.VMEM((rhs, K, LANES), F32),
        pltpu.VMEM((half, K, LANES), F32),
    ]
    *upward, up1, up2, up3 = pl.pallas_call(
        first_kernel,
        out_shape=up_shapes
        + (shape((K, K, leaves)), shape((K, K, LANES)), shape((K, K, LANES))),
        grid=(1,),
        in_specs=[whole(a) for a in (right_sides, leaf_basis, transfer_first, transfer_second, transfer_third)],
        out_specs=(VM,) * 6,
        scratch_shapes=up_scratch,
        compiler_params=params(56),
        cost_estimate=cost(FIRST * 10**9, 3 * 2**20),
    )(right_sides, leaf_basis, transfer_first, transfer_second, transfer_third)
    vectors, basis, blocks = right_sides, leaf_basis, near_blocks
    cut = order // PIECES

    def prepare(up1, up2, up3):
        return pl.pallas_call(
            prep_rest_kernel,
            out_shape=(
                shape((K, K, leaves)), shape((K, K, LANES)), shape((K, K, LANES)),
                shape((NC, K, K, LANES)), shape((NC, K, K, LANES)),
                shape((NFAR * top_coupling.shape[3] // LANES, K, K, LANES)), shape((NC, K, K, LANES)),
            ),
            in_specs=[VM] * 6,
            out_specs=(VM,) * 7,
            scratch_shapes=[pltpu.VMEM((K * K, LANES), F32)],
            compiler_params=params(16),
            cost_estimate=cost(10**9, 9 * 2**20),
        )(up1, up2, up3, coupling_first, coupling_second, top_coupling)

    def near_piece(i, vectors):
        return pl.pallas_call(
            functools.partial(near_kernel, i * cut // CHUNK),
            out_shape=shape((rhs, cut), F32),
            in_specs=[SM, VM, VM],
            out_specs=VM,
            scratch_shapes=[pltpu.VMEM((leaves + 2 * HN, rhs, LANES), BF16)],
            compiler_params=params(16),
            cost_estimate=cost(10**9, 8 * 2**20),
        )(near_local, vectors, blocks)

    def couple(coef1, coef2, m1, m2):
        return pl.pallas_call(
            couple_kernel,
            out_shape=(shape((rhs, K, LANES), F32), shape((half, K, LANES), F32)),
            in_specs=[SM] + [VM] * 6,
            out_specs=(VM,) * 2,
            scratch_shapes=[pltpu.VMEM((rhs, NC * K, LANES), F32)],
            compiler_params=params(16),
            cost_estimate=cost(10**9, 8 * 2**20),
        )(me, coef1, coef2, lists[0], lists[1], m1, m2)

    def exchange(sent, works):
        every, done = sent[None], []
        for step, b in enumerate(reversed(range(bits))):
            pairs = [(i, i ^ (1 << b)) for i in range(devices)]
            other = lax.ppermute(every, AXES, pairs)
            if step < len(works):
                result = works[step](every)
                other, result = lax.optimization_barrier((other, result))
                done.append(result)
            if b:
                every = jnp.concatenate([every, other], axis=0)
        return every, other, done

    def held(values, every):
        return lax.optimization_barrier((*values, every))[:-1]

    def down(every, other, far1, far2, vectors, nears, prepared, keep):
        d1, d2, d3, _, _, m3, ends = prepared
        out = shape((rhs, order))
        results = pl.pallas_call(
            functools.partial(down_kernel, bits),
            out_shape=(out, out) if keep else (out,),
            in_specs=[SM, SM] + [VM] * 5 + [VM] * PIECES + [VM] * 10,
            out_specs=(HBM, VM) if keep else (HBM,),
            scratch_shapes=([] if keep else [pltpu.VMEM((rhs, order), BF16)])
            + [
                pltpu.VMEM((rhs * K, devices * (leaves // 8)), BF16),
                pltpu.VMEM((rhs, NFAR * K * (leaves // 8) // LANES, LANES), F32),
                pltpu.VMEM((rhs, K, LANES), F32),
                pltpu.VMEM((rhs, K, LANES), F32),
                pltpu.VMEM((leaves // LANES, rhs, K, LANES), F32),
                pltpu.VMEM((leaves // 4 * rhs, LANES), F32),
                pltpu.VMEM((16, rhs, LANES), BF16),
                pltpu.SemaphoreType.DMA((4,)),
            ],
            compiler_params=params(24),
            cost_estimate=cost(10**9, 8 * 2**20),
        )(me, near_local, every, other, far1, far2, vectors, *nears, blocks, basis, *lists, ends, m3, d1, d2, d3)
        return results

    sent, coef1, coef2 = upward
    prepared = []
    works = [
        lambda every: near_piece(0, *held((vectors,), every)),
        lambda every: prepared.extend(prepare(*held((up1, up2, up3), every))) or tuple(prepared),
        lambda every: couple(*held((coef1, coef2), every), *prepared[3:5]),
        lambda every: near_piece(1, *held((vectors,), every)),
    ]
    every, other, (near0, prepared, fars, near1) = exchange(sent, works)
    first_image, second_vectors = down(every, other, *fars, vectors, (near0, near1), prepared, True)
    sent, coef1, coef2 = pl.pallas_call(
        up_kernel,
        out_shape=up_shapes,
        in_specs=[VM] * 5,
        out_specs=(VM,) * 3,
        scratch_shapes=up_scratch,
        compiler_params=params(12),
        cost_estimate=cost(10**8, 3 * 2**20),
    )(second_vectors, basis, up1, up2, up3)
    works = [
        lambda every: near_piece(0, *held((second_vectors,), every)),
        lambda every: near_piece(1, *held((second_vectors,), every)),
        lambda every: couple(*held((coef1, coef2), every), *prepared[3:5]),
    ]
    every, other, (near0, near1, fars) = exchange(sent, works)
    (second_image,) = down(every, other, *fars, second_vectors, (near0, near1), prepared, False)
    return (first_image, second_image)


def solution(mesh):
    tree = P(None, None, AXES)
    placed = (
        P("groups", AXES), tree, P(AXES, None), P(None, AXES), tree, tree, tree,
        P(None, None, None, AXES), P(None, None, None, AXES), P(AXES, None), P(AXES, None),
        P(None, None, None, AXES), P(AXES, None),
    )
    return jax.shard_map(
        body, mesh=mesh, in_specs=placed, out_specs=(P("groups", AXES), P("groups", AXES)), check_vma=False
    )
```

```python
import functools

import jax
import jax.numpy as jnp
from jax import lax
from jax.experimental import pallas as pl
from jax.experimental.pallas import tpu as pltpu
from jax.sharding import PartitionSpec as P

M = 64
K = 32
NEAR = 5
NC = 3
NFAR = 8
HN = 2
HC = 2
LANES = 128
AXES = ("branch", "sub")
PIECES = 2
UNROLL = 32
FIRST = 1
CHUNK = 1024
F32 = jnp.float32
BF16 = jnp.bfloat16
NT = (((1,), (1,)), ((), ()))


def iota(shape, dim):
    return lax.broadcasted_iota(jnp.int32, shape, dim)


def place(node, count, levels):
    where = jnp.zeros_like(node)
    for level in range(levels):
        count //= 2
        where = where + (node & 1) * count
        node = node >> 1
    return where + node


def place_static(node, count, levels):
    where = 0
    for level in range(levels):
        count //= 2
        where += (node & 1) * count
        node >>= 1
    return where + node


def lane_order(count, levels, copies=1):
    rows = place(iota((count, count * copies), 0), count, levels)
    columns = iota((count, count * copies), 1) & (count - 1)
    return jnp.where(rows == columns, 1.0, 0.0).astype(BF16)


def dot(a, b):
    return jnp.dot(a, b, preferred_element_type=F32)


def end_nodes(count):
    return (0, 1, count - 2, count - 1)


def end_columns(count, offset):
    row, lane = iota((count, LANES), 0), iota((count, LANES), 1) & 7
    hit = row < 0
    for e, node in enumerate(end_nodes(count)):
        hit = hit | ((row == node) & (lane == offset + e))
    return jnp.where(hit, 1.0, 0.0).astype(BF16)


def rounded(x):
    return x.astype(BF16).astype(F32)


def contract(terms, init, lanes):
    def step(position, accs):
        for matrix_at, x_at in terms:
            matrix = matrix_at(position).astype(F32)
            accs = tuple(acc + matrix * x_at(r, position) for r, acc in enumerate(accs))
        return accs

    return lax.fori_loop(0, K, step, init, unroll=UNROLL)


def prep_up_kernel(first_ref, second_ref, third_ref, up1_ref, up2_ref, up3_ref):
    for source, target, levels, copies in ((first_ref, up1_ref, 3, 1), (second_ref, up2_ref, 2, 1), (third_ref, up3_ref, 1, 2)):
        count = source.shape[2]
        order = lane_order(count, levels, copies)
        for k in range(0, K, 4):
            rows = source[k : k + 4].reshape(4 * K, count)
            target[k : k + 4] = dot(rows, order).astype(BF16).reshape(4, K, count * copies)


def prep_rest_kernel(up1_ref, up2_ref, up3_ref, c1_ref, c2_ref, c3_ref, d1_ref, d2_ref, d3_ref, m1_ref, m2_ref, m3_ref, ends_ref, wide_ref):
    for source, target in ((up1_ref, d1_ref), (up2_ref, d2_ref), (up3_ref, d3_ref)):
        for tile in range(source.shape[2] // LANES):
            lanes = slice(tile * LANES, (tile + 1) * LANES)
            wide_ref[...] = source[:, :, lanes].astype(F32).reshape(K * K, LANES)
            for m in range(K):
                target[m, :, lanes] = wide_ref[pl.ds(m, K, stride=K), :].astype(BF16)
    for source, target, levels, copies in ((c1_ref, m1_ref, 2, 1), (c2_ref, m2_ref, 1, 2)):
        count = source.shape[3]
        order = lane_order(count, levels, copies)
        for j in range(NC):
            for k in range(0, K, 8):
                rows = source[j, k : k + 8].reshape(8 * K, count)
                target[j, k : k + 8] = dot(rows, order).astype(BF16).reshape(8, K, LANES)
    low_ends = end_columns(LANES, 0)
    high_ends = end_columns(M, 4)
    for j in range(NC):
        for k in range(0, K, 8):
            low = dot(c1_ref[j, k : k + 8].reshape(8 * K, LANES), low_ends)
            high = dot(c2_ref[j, k : k + 8].reshape(8 * K, M), high_ends)
            ends_ref[j, k : k + 8] = (low + high).astype(BF16).reshape(8, K, LANES)
    top = c3_ref.shape[3]
    group = LANES // top
    for h in range(NFAR // group):
        for k in range(0, K, 8):
            total = None
            for q in range(group):
                put = jnp.where(iota((top, LANES), 0) + q * top == iota((top, LANES), 1), 1.0, 0.0).astype(BF16)
                part = dot(c3_ref[h * group + q, k : k + 8].reshape(8 * K, top), put)
                total = part if total is None else total + part
            m3_ref[h, k : k + 8] = total.astype(BF16).reshape(8, K, LANES)


def spread_basis(part):
    low = iota((K, LANES), 1) < M
    zero = jnp.zeros((K, LANES), BF16)
    left, right = part[:, :LANES], part[:, LANES:]
    first = jnp.concatenate([jnp.where(low, left, zero), jnp.where(low, zero, left), zero, zero], axis=0)
    second = jnp.concatenate([zero, zero, jnp.where(low, right, zero), jnp.where(low, zero, right)], axis=0)
    return jnp.concatenate([first, second], axis=1)


def up_kernel(z_ref, basis_ref, up1_ref, up2_ref, up3_ref, sent_ref, coef1_ref, coef2_ref, rows_ref, x0_ref, x1_ref, x2_ref):
    rhs, order = z_ref.shape
    leaves = order // M
    top = leaves // 8
    groups = leaves // 4
    for g in range(groups):
        lanes = slice(g * 256, (g + 1) * 256)
        rows_ref[g * rhs : (g + 1) * rhs] = lax.dot_general(
            z_ref[:, lanes], spread_basis(basis_ref[:, lanes]), NT, preferred_element_type=F32
        )
    unit = jnp.where(iota((LANES, LANES), 0) == iota((LANES, LANES), 1), 1.0, 0.0).astype(BF16)
    for r in range(rhs):
        pieces = [rows_ref[pl.ds(a * rhs + r, top, stride=2 * rhs), :] for a in range(2)]
        flat = jnp.concatenate(pieces, axis=0).astype(BF16)
        both = jnp.concatenate([flat, flat], axis=0)
        tall = lax.dot_general(unit, both, NT, preferred_element_type=F32)
        keep = iota((K, LANES), 1) < M
        for c in range(2):
            x0_ref[c, r] = jnp.where(keep, tall[c * K : (c + 1) * K], tall[(2 + c) * K : (3 + c) * K])

    half = rhs // 2
    zeros = tuple(jnp.zeros((K, LANES), F32) for _ in range(half))
    for first in (0, half):
        terms = [
            (
                functools.partial(lambda s, k: up1_ref[k, :, s * LANES : (s + 1) * LANES], s),
                functools.partial(lambda s, r, k: x0_ref[s, first + r, pl.ds(k, 1), :], s),
            )
            for s in range(2)
        ]
        for r, acc in enumerate(contract(terms, zeros, LANES)):
            coef1_ref[first + r] = acc.astype(BF16)
            x1_ref[first + r] = rounded(acc)
    low = iota((K, LANES), 1) < M
    for first in (0, half):
        terms = [(lambda k: up2_ref[k], lambda r, k: x1_ref[first + r, pl.ds(k, 1), :])]
        for r, acc in enumerate(contract(terms, zeros, LANES)):
            total = rounded(acc + pltpu.roll(acc, 64, 1))
            if first == 0:
                x2_ref[r] = total
            else:
                both = jnp.where(low, x2_ref[r], total)
                x2_ref[r] = both
                coef2_ref[r] = both.astype(BF16)
    terms = [(lambda k: up3_ref[k], lambda r, k: x2_ref[r, pl.ds(k, 1), :])]
    sums = [acc + pltpu.roll(acc, 32, 1) for acc in contract(terms, zeros, LANES)]
    odd = (iota((K, LANES), 1) & 32) > 0
    for r in range(half // 2):
        sent_ref[r * K : (r + 1) * K] = jnp.where(odd, sums[r], pltpu.roll(sums[r + half // 2], 96, 1)).astype(BF16)

    def ends(count, offset, shift):
        row, column = iota((LANES, LANES), 0), iota((LANES, LANES), 1)
        hit = (row == -1)
        for copy in range(LANES // count):
            for e, node in enumerate((0, 1, count - 2, count - 1)):
                at = place_static(node, count, 2 if count == LANES else 1)
                hit = hit | ((row == copy * count + at) & (column == copy * M + offset + e))
        return jnp.where(hit, 1.0, 0.0).astype(BF16)

    first_ends = dot(x1_ref[...].astype(BF16).reshape(rhs * K, LANES), ends(LANES, 0, 0)).reshape(rhs, K, LANES)
    second_ends = dot(x2_ref[...].astype(BF16).reshape(half * K, LANES), ends(M, 4, 64)).reshape(half, K, LANES)
    packed = jnp.zeros((K, LANES), F32)
    for r in range(rhs):
        value = first_ends[r]
        if r < half:
            value = value + second_ends[r]
        packed = packed + (pltpu.roll(value, 8 * r, 1) if r else value)
    base = half // 2 * K
    sent_ref[base : base + K] = packed.astype(BF16)
    sent_ref[base + K : base + K + rhs] = z_ref[:, :LANES]
    sent_ref[base + K + rhs : base + K + 2 * rhs] = z_ref[:, order - LANES :]


def first_kernel(
    z_hbm, basis_hbm, first_hbm, second_hbm, third_hbm,
    sent_ref, coef1_ref, coef2_ref, up1_ref, up2_ref, up3_ref,
    z_ref, basis_ref, first_ref, second_ref, third_ref, sems, *scratch
):
    sources = (first_hbm, second_hbm, third_hbm, z_hbm, basis_hbm)
    targets = (first_ref, second_ref, third_ref, z_ref, basis_ref)
    copies = [pltpu.make_async_copy(a, b, sems.at[i]) for i, (a, b) in enumerate(zip(sources, targets))]
    for copy in copies:
        copy.start()
    for copy in copies[:3]:
        copy.wait()
    prep_up_kernel(first_ref, second_ref, third_ref, up1_ref, up2_ref, up3_ref)
    for copy in copies[3:]:
        copy.wait()
    up_kernel(z_ref, basis_ref, up1_ref, up2_ref, up3_ref, sent_ref, coef1_ref, coef2_ref, *scratch)


def put_leaves(target_ref, tile, slot):
    low = iota(tile.shape, 1) < M
    wide = tile.astype(F32)
    swapped = pltpu.roll(wide, M, 1)
    target_ref[slot] = jnp.where(low, wide, swapped).astype(BF16)
    target_ref[slot + 1] = jnp.where(low, swapped, wide).astype(BF16)


def own_blocks(res, rhs):
    low = iota((rhs, LANES), 1) < M
    return jnp.concatenate(
        [
            jnp.where(low, res[:rhs, :LANES], res[rhs : 2 * rhs, :LANES]),
            jnp.where(low, res[2 * rhs : 3 * rhs, LANES:], res[3 * rhs :, LANES:]),
        ],
        axis=1,
    )


def near_group(read, weights, rhs):
    low = iota((rhs, LANES), 1) < M
    rows = []
    for leaf in range(4):
        z = [read(j, leaf) for j in range(NEAR)]
        rows.append(jnp.concatenate([jnp.where(low, z[0], z[1]), jnp.where(low, z[2], z[3]), z[4][:, :M]], axis=1))
    return own_blocks(dot(jnp.concatenate(rows, axis=0), weights), rhs)


def near_kernel(chunk0, leaves_ref, z_ref, blocks_ref, out_ref, z_leaves_ref):
    rhs, order = z_ref.shape
    chunks = out_ref.shape[1] // CHUNK
    per = CHUNK // M
    first_tile = max(chunk0 * (CHUNK // LANES) - 1, 0)
    last_tile = min((chunk0 + chunks) * (CHUNK // LANES) + 1, order // LANES)
    for t in range(first_tile, last_tile):
        put_leaves(z_leaves_ref, z_ref[:, t * LANES : (t + 1) * LANES], 2 * t + HN)

    @pl.loop(0, chunks)
    def _(c):
        for g in range(CHUNK // 256):
            leaf0 = (chunk0 + c) * per + 4 * g
            here = pl.ds(pl.multiple_of(c * CHUNK + g * 256, 256), 256)
            there = pl.ds(pl.multiple_of((chunk0 + c) * CHUNK + g * 256, 256), 256)
            weights = blocks_ref[:, :, there].reshape(NEAR * M, 256)
            out_ref[:, here] = near_group(lambda j, e: z_leaves_ref[leaves_ref[j, leaf0 + e]], weights, rhs)


def bit_reverse(value, bits):
    out = jnp.zeros_like(value)
    for b in range(bits):
        out = out + (((value >> b) & 1) << (bits - 1 - b))
    return out


def in_order(rows, count, levels):
    wide = jnp.concatenate([rows.astype(F32)] + [jnp.zeros((8 - rows.shape[0], count), F32)], axis=0).astype(BF16)
    return dot(wide, lane_order(count, levels)).astype(jnp.int32)


def own_rows_of(nodes, me, count, levels):
    local = nodes - me * count
    inside = (local >= 0) & (local < count)
    return in_order(jnp.where(inside, place(jnp.clip(local, 0, count - 1), count, levels), -1), count, levels)


def couple_kernel(
    bits, me_ref, coef1_ref, coef2_ref, list1_ref, list2_ref, top_ref, m1_ref, m2_ref, far1_ref, far2_ref, table_ref, picks_ref
):
    rhs, half = coef1_ref.shape[0], coef2_ref.shape[0]
    me = me_ref[0]
    devices, top = 1 << bits, top_ref.shape[1]
    per = LANES // top
    nodes = top_ref[...]
    rows = bit_reverse(jnp.bitwise_xor(nodes // top, me), bits) * top + nodes % top
    hot = []
    for j in range(NFAR):
        hot.append(jnp.where(iota((devices * top, top), 0) == rows[j : j + 1], 1.0, 0.0).astype(BF16))
    for h in range(NFAR // per):
        wide = None
        for q in range(per):
            put = jnp.where(iota((top, LANES), 0) + q * top == iota((top, LANES), 1), 1.0, 0.0).astype(BF16)
            part = dot(hot[h * per + q], put)
            wide = part if wide is None else wide + part
        table_ref[h] = wide.astype(BF16)
    zeros = tuple(jnp.zeros((K, LANES), F32) for _ in range(half))

    def run(matrix_ref, first):
        terms = [
            (
                functools.partial(lambda j, k: matrix_ref[j, k], j),
                functools.partial(lambda j, r, k: picks_ref[first + r, pl.ds(j * K + k, 1), :], j),
            )
            for j in range(NC)
        ]
        return contract(terms, zeros, LANES)

    rows = own_rows_of(list2_ref[...], me, M, 1)
    copy_of = iota((LANES, LANES), 1) // M
    tables = []
    for j in range(NC):
        row = jnp.concatenate([rows[j : j + 1], rows[j : j + 1]], axis=1)
        tables.append(jnp.where((iota((LANES, LANES), 0) - copy_of * M == row) & (row >= 0), 1.0, 0.0))
    table = jnp.concatenate(tables, axis=1).astype(BF16)
    picked = dot(coef2_ref[...].reshape(half * K, LANES), table).reshape(half, K, NC * LANES)
    for j in range(NC):
        picks_ref[:half, j * K : (j + 1) * K, :] = picked[:, :, j * LANES : (j + 1) * LANES]
    for r, acc in enumerate(run(m2_ref, 0)):
        far2_ref[r] = acc
    rows = own_rows_of(list1_ref[...], me, LANES, 2)
    table = jnp.concatenate(
        [jnp.where(iota((LANES, LANES), 0) == rows[j : j + 1], 1.0, 0.0) for j in range(NC)], axis=1
    ).astype(BF16)
    picked = dot(coef1_ref[...].reshape(rhs * K, LANES), table).reshape(rhs, K, NC * LANES)
    for j in range(NC):
        picks_ref[:, j * K : (j + 1) * K, :] = picked[:, :, j * LANES : (j + 1) * LANES]
    for first in (0, half):
        for r, acc in enumerate(run(m1_ref, first)):
            far1_ref[first + r] = acc


def halo_codes(nodes, me, count, offset):
    local = nodes - me * count
    code = jnp.where(local < 0, local + 5, jnp.where(local >= count, local - count + 1, 0))
    code = jnp.where(code > 0, code + offset, 0)
    wide = jnp.concatenate([code.astype(F32)] + [jnp.zeros((8 - code.shape[0], count), F32)], axis=0).astype(BF16)
    return dot(wide, end_columns(count, offset))


def down_kernel(bits, me_ref, leaves_ref, early_ref, late_ref, far1_in_ref, far2_in_ref, z_ref, *refs):
    near_refs = refs[:PIECES]
    (blocks_ref, basis_ref, list1_ref, list2_ref, table_ref, ends_ref, m3_ref, d1_ref, d2_ref, d3_ref,
     out_hbm, out_ref, every_ref, picks_ref, far1_ref, x_ref, x0_ref, rows_ref, z_leaves_ref, sems) = refs[PIECES:]
    rhs, order = z_ref.shape
    leaves = order // M
    top = leaves // 8
    half = rhs // 2
    me = me_ref[0]
    devices = 1 << bits
    own_rows = half // 2 * K

    def block(device, rows):
        at = bit_reverse(jnp.bitwise_xor(device, me), bits)
        early = early_ref[jnp.minimum(at, devices // 2 - 1), rows]
        late = late_ref[jnp.maximum(at - devices // 2, 0), rows]
        return jnp.where(at < devices // 2, early.astype(F32), late.astype(F32))

    before = jnp.maximum(me - 1, 0)
    after = jnp.minimum(me + 1, devices - 1)

    z_before = block(before, slice(own_rows + K + rhs, own_rows + K + 2 * rhs)).astype(BF16)
    z_after = block(after, slice(own_rows + K, own_rows + K + rhs)).astype(BF16)
    put_leaves(z_leaves_ref, z_before, 0)
    for t in range(3):
        put_leaves(z_leaves_ref, z_ref[:, t * LANES : (t + 1) * LANES], 2 + 2 * t)
        put_leaves(z_leaves_ref, z_ref[:, order - (3 - t) * LANES : order - (2 - t) * LANES or None], 8 + 2 * t)
    put_leaves(z_leaves_ref, z_after, 14)
    head = near_group(lambda j, e: z_leaves_ref[leaves_ref[j, e]], blocks_ref[:, :, :256].reshape(NEAR * M, 256), rhs)
    skip = leaves + 2 * HN - 16
    tail = near_group(
        lambda j, e: z_leaves_ref[leaves_ref[j, leaves - 4 + e] - skip], blocks_ref[:, :, order - 256 :].reshape(NEAR * M, 256), rhs
    )

    sides = slice(own_rows, own_rows + K)
    halo = jnp.where((iota((K, LANES), 1) & 2) > 0, block(before, sides), block(after, sides)).astype(BF16)
    codes = (halo_codes(list1_ref[...], me, LANES, 0) + halo_codes(list2_ref[...], me, M, 4)).astype(jnp.int32)
    lane_group = iota((LANES, LANES), 1) & -8
    sums = []
    for j in range(NC):
        code = codes[j : j + 1]
        table = jnp.where((iota((LANES, LANES), 0) == lane_group + code - 1) & (code > 0), 1.0, 0.0).astype(BF16)
        x_ref[j] = dot(halo, table)
    for j in range(NC):
        total = jnp.zeros((K, LANES), F32)
        for k in range(K):
            total = total + ends_ref[j, k].astype(F32) * x_ref[j, k : k + 1, :]
        sums.append(total)
    outer = sums[0] + sums[1] + sums[2]
    turned = jnp.concatenate([pltpu.roll(outer, LANES - 8 * r, 1) if r else outer for r in range(rhs)], axis=0)
    coarse = turned.astype(BF16)
    fine = (turned - coarse.astype(F32)).astype(BF16)

    def scatter(count, offset):
        row, column = iota((LANES, LANES), 0), iota((LANES, LANES), 1)
        hit = row < 0
        for copy in range(LANES // count):
            for e, node in enumerate(end_nodes(count)):
                at = place_static(node, count, 2 if count == LANES else 1)
                hit = hit | ((column == copy * count + at) & (row == copy * M + offset + e))
        return jnp.where(hit, 1.0, 0.0).astype(BF16)

    put = scatter(LANES, 0)
    outer1 = (dot(coarse, put) + dot(fine, put)).reshape(rhs, K, LANES)
    put = scatter(M, 4)
    outer2 = (dot(coarse[: half * K], put) + dot(fine[: half * K], put)).reshape(half, K, LANES)

    group = iota((own_rows, LANES), 1) // top
    per = LANES // top
    for tile in range(devices // per):
        source = early_ref if tile < devices // per // 2 else late_ref
        first = tile * per - (0 if tile < devices // per // 2 else devices // 2)
        parts = [source[first + q, :own_rows].astype(F32) for q in range(per)]
        for g in range(per):
            merged = None
            for q in range(per):
                shift = (q - g) * top % LANES
                moved = pltpu.roll(parts[q], shift, 1) if shift else parts[q]
                merged = moved if merged is None else jnp.where(group == q, moved, merged)
            every_ref[g * own_rows : (g + 1) * own_rows, tile * LANES : (tile + 1) * LANES] = merged.astype(BF16)
    for h in range(NFAR // per):
        picked = dot(every_ref[...], table_ref[h])
        picks_ref[:, h * K : (h + 1) * K, :] = picked.reshape(rhs, K, LANES)
    zeros = tuple(jnp.zeros((K, LANES), F32) for _ in range(half))
    groups_of = [1, 0, 3, 2]

    def slot(r):
        quarter = rhs // 4
        return groups_of[r // quarter] * quarter + r % quarter

    low = iota((K, LANES), 1) < M
    kept = {}
    for first in range(0, rhs, half):
        terms = [
            (
                functools.partial(lambda h, k: m3_ref[h, k], h),
                functools.partial(lambda h, r, k: picks_ref[slot(first + r), pl.ds(h * K + k, 1), :], h),
            )
            for h in range(NFAR // per)
        ]
        for r, acc in enumerate(contract(terms, zeros, LANES)):
            acc = acc + pltpu.roll(acc, 64, 1)
            acc = rounded(acc + pltpu.roll(acc, 32, 1))
            if first == 0:
                x_ref[r] = acc
            else:
                x_ref[r] = jnp.where(low, x_ref[r], acc)

    terms = [(lambda m: d3_ref[m], lambda r, m: x_ref[r, pl.ds(m, 1), :])]
    start = tuple(far2_in_ref[r] + outer2[r] for r in range(half))
    for r, acc in enumerate(contract(terms, start, LANES)):
        value = rounded(acc)
        swapped = pltpu.roll(value, M, 1)
        x_ref[r] = jnp.where(low, value, swapped)
        x_ref[r + half] = jnp.where(low, swapped, value)

    for first in (0, half):
        terms = [(lambda m: d2_ref[m], lambda r, m: x_ref[first + r, pl.ds(m, 1), :])]
        start = tuple(far1_in_ref[first + r] + outer1[first + r] for r in range(half))
        for r, acc in enumerate(contract(terms, start, LANES)):
            far1_ref[first + r] = rounded(acc)

    for first in (0, half):
        for s in range(2):
            lanes = slice(s * LANES, (s + 1) * LANES)
            terms = [(lambda m: d1_ref[m, :, lanes], lambda r, m: far1_ref[first + r, pl.ds(m, 1), :])]
            for r, acc in enumerate(contract(terms, zeros, LANES)):
                x0_ref[s, first + r] = acc
    groups = leaves // 4
    node = iota((LANES, LANES), 0) & (groups - 1)
    lane = (iota((LANES, LANES), 0) & -groups) + (node & 1) * top + (node >> 1)
    turn = jnp.where(lane == iota((LANES, LANES), 1), 1.0, 0.0).astype(BF16)
    for r in range(rhs):
        flat = jnp.concatenate([x0_ref[0, r], x0_ref[1, r]], axis=0).astype(BF16)
        both = jnp.concatenate([flat, flat], axis=0)
        tall = lax.dot_general(turn, both, NT, preferred_element_type=F32)
        keep = iota((groups, LANES), 1) < M
        rows_ref[pl.ds(r, groups, stride=rhs), :] = jnp.where(keep, tall[:groups], tall[groups:])

    def far_group(g):
        lanes = slice(g * 256, (g + 1) * 256)
        coefs = rows_ref[g * rhs : (g + 1) * rhs].astype(BF16)
        return dot(coefs, spread_basis(basis_ref[:, lanes]))

    total = leaves // 4
    parts = 4
    for part in range(parts):
        inside = range(part * total // parts, (part + 1) * total // parts)
        fars = [far_group(g) for g in inside]
        for g, far in zip(inside, fars):
            if g == 0:
                near = head
            elif g == total - 1:
                near = tail
            else:
                at = 0
                while g * 256 >= at + near_refs[0].shape[1]:
                    at += near_refs[0].shape[1]
                near = near_refs[at // near_refs[0].shape[1]][:, g * 256 - at : (g + 1) * 256 - at]
            out_ref[:, g * 256 : (g + 1) * 256] = (near + far).astype(BF16)
        lanes = slice(part * order // parts, (part + 1) * order // parts)
        pltpu.make_async_copy(out_ref.at[:, lanes], out_hbm.at[:, lanes], sems.at[part]).start()
    for part in range(parts):
        lanes = slice(part * order // parts, (part + 1) * order // parts)
        pltpu.make_async_copy(out_ref.at[:, lanes], out_hbm.at[:, lanes], sems.at[part]).wait()


VM = pl.BlockSpec(memory_space=pltpu.VMEM)
SM = pl.BlockSpec(memory_space=pltpu.SMEM)
HBM = pl.BlockSpec(memory_space=pltpu.HBM)


def params(mib):
    return pltpu.CompilerParams(vmem_limit_bytes=mib * 2**20)


def cost(flops, moved):
    return pl.CostEstimate(flops=flops, bytes_accessed=moved, transcendentals=0)


def shape(dims, kind=BF16):
    return jax.ShapeDtypeStruct(dims, kind)


def body(
    right_sides, near_blocks, near_leaves, leaf_basis, transfer_first, transfer_second, transfer_third,
    coupling_first, coupling_second, list_first, list_second, top_coupling, top_nodes,
):
    position = lax.axis_index(AXES)
    devices = lax.axis_size("branch") * lax.axis_size("sub")
    bits = devices.bit_length() - 1
    rhs, order = right_sides.shape
    leaves = order // M
    half = rhs // 2
    me = position.astype(jnp.int32).reshape(1)
    near_local = near_leaves.T - (position * leaves - HN)
    lists = (list_first.T, list_second.T, top_nodes.T)

    sent_rows = half // 2 * K + K + 2 * rhs
    up_shapes = (shape((sent_rows, LANES)), shape((rhs, K, LANES)), shape((half, K, LANES)))
    up_scratch = [
        pltpu.VMEM((leaves // 4 * rhs, LANES), F32),
        pltpu.VMEM((leaves // LANES, rhs, K, LANES), F32),
        pltpu.VMEM((rhs, K, LANES), F32),
        pltpu.VMEM((half, K, LANES), F32),
    ]
    *upward, up1, up2, up3 = pl.pallas_call(
        first_kernel,
        out_shape=up_shapes
        + (shape((K, K, leaves)), shape((K, K, LANES)), shape((K, K, LANES))),
        in_specs=[HBM] * 5,
        out_specs=(VM,) * 6,
        scratch_shapes=[
            pltpu.VMEM(a.shape, BF16)
            for a in (right_sides, leaf_basis, transfer_first, transfer_second, transfer_third)
        ]
        + [pltpu.SemaphoreType.DMA((5,))]
        + up_scratch,
        compiler_params=params(56),
        cost_estimate=cost(FIRST * 10**9, 3 * 2**20),
    )(right_sides, leaf_basis, transfer_first, transfer_second, transfer_third)
    vectors, basis, blocks = right_sides, leaf_basis, near_blocks
    cut = order // PIECES

    def prepare(up1, up2, up3):
        return pl.pallas_call(
            prep_rest_kernel,
            out_shape=(
                shape((K, K, leaves)), shape((K, K, LANES)), shape((K, K, LANES)),
                shape((NC, K, K, LANES)), shape((NC, K, K, LANES)),
                shape((NFAR * top_coupling.shape[3] // LANES, K, K, LANES)), shape((NC, K, K, LANES)),
            ),
            in_specs=[VM] * 6,
            out_specs=(VM,) * 7,
            scratch_shapes=[pltpu.VMEM((K * K, LANES), F32)],
            compiler_params=params(16),
            cost_estimate=cost(10**9, 9 * 2**20),
        )(up1, up2, up3, coupling_first, coupling_second, top_coupling)

    def near_piece(i, vectors):
        return pl.pallas_call(
            functools.partial(near_kernel, i * cut // CHUNK),
            out_shape=shape((rhs, cut), F32),
            in_specs=[SM, VM, VM],
            out_specs=VM,
            scratch_shapes=[pltpu.VMEM((leaves + 2 * HN, rhs, LANES), BF16)],
            compiler_params=params(16),
            cost_estimate=cost(10**9, 8 * 2**20),
        )(near_local, vectors, blocks)

    def couple(coef1, coef2, m1, m2):
        return pl.pallas_call(
            functools.partial(couple_kernel, bits),
            out_shape=(
                shape((rhs, K, LANES), F32), shape((half, K, LANES), F32),
                shape((NFAR * (leaves // 8) // LANES, devices * (leaves // 8), LANES)),
            ),
            in_specs=[SM] + [VM] * 7,
            out_specs=(VM,) * 3,
            scratch_shapes=[pltpu.VMEM((rhs, NC * K, LANES), F32)],
            compiler_params=params(16),
            cost_estimate=cost(10**9, 8 * 2**20),
        )(me, coef1, coef2, *lists, m1, m2)

    def exchange(sent, works):
        every, done = sent[None], []
        for step, b in enumerate(reversed(range(bits))):
            pairs = [(i, i ^ (1 << b)) for i in range(devices)]
            other = lax.ppermute(every, AXES, pairs)
            if step < len(works):
                result = works[step](every)
                other, result = lax.optimization_barrier((other, result))
                done.append(result)
            if b:
                every = jnp.concatenate([every, other], axis=0)
        return every, other, done

    def held(values, every):
        return lax.optimization_barrier((*values, every))[:-1]

    def down(every, other, far1, far2, table, vectors, nears, prepared, keep):
        d1, d2, d3, _, _, m3, ends = prepared
        out = shape((rhs, order))
        results = pl.pallas_call(
            functools.partial(down_kernel, bits),
            out_shape=(out, out) if keep else (out,),
            in_specs=[SM, SM] + [VM] * 5 + [VM] * PIECES + [VM] * 10,
            out_specs=(HBM, VM) if keep else (HBM,),
            scratch_shapes=([] if keep else [pltpu.VMEM((rhs, order), BF16)])
            + [
                pltpu.VMEM((rhs * K, devices * (leaves // 8)), BF16),
                pltpu.VMEM((rhs, NFAR * K * (leaves // 8) // LANES, LANES), F32),
                pltpu.VMEM((rhs, K, LANES), F32),
                pltpu.VMEM((rhs, K, LANES), F32),
                pltpu.VMEM((leaves // LANES, rhs, K, LANES), F32),
                pltpu.VMEM((leaves // 4 * rhs, LANES), F32),
                pltpu.VMEM((16, rhs, LANES), BF16),
                pltpu.SemaphoreType.DMA((4,)),
            ],
            compiler_params=params(24),
            cost_estimate=cost(10**9, 8 * 2**20),
        )(me, near_local, every, other, far1, far2, vectors, *nears, blocks, basis, *lists[:2], table, ends, m3, d1, d2, d3)
        return results

    sent, coef1, coef2 = upward
    prepared = []
    works = [
        lambda every: near_piece(0, *held((vectors,), every)),
        lambda every: prepared.extend(prepare(*held((up1, up2, up3), every))) or tuple(prepared),
        lambda every: couple(*held((coef1, coef2), every), *prepared[3:5]),
        lambda every: near_piece(1, *held((vectors,), every)),
    ]
    every, other, (near0, prepared, fars, near1) = exchange(sent, works)
    first_image, second_vectors = down(every, other, *fars, vectors, (near0, near1), prepared, True)
    sent, coef1, coef2 = pl.pallas_call(
        up_kernel,
        out_shape=up_shapes,
        in_specs=[VM] * 5,
        out_specs=(VM,) * 3,
        scratch_shapes=up_scratch,
        compiler_params=params(12),
        cost_estimate=cost(10**8, 3 * 2**20),
    )(second_vectors, basis, up1, up2, up3)
    works = [
        lambda every: couple(*held((coef1, coef2), every), *prepared[3:5]),
        lambda every: near_piece(0, *held((second_vectors,), every)),
        lambda every: near_piece(1, *held((second_vectors,), every)),
    ]
    every, other, (fars, near0, near1) = exchange(sent, works)
    (second_image,) = down(every, other, *fars, second_vectors, (near0, near1), prepared, False)
    return (first_image, second_image)


def solution(mesh):
    tree = P(None, None, AXES)
    placed = (
        P("groups", AXES), tree, P(AXES, None), P(None, AXES), tree, tree, tree,
        P(None, None, None, AXES), P(None, None, None, AXES), P(AXES, None), P(AXES, None),
        P(None, None, None, AXES), P(AXES, None),
    )
    return jax.shard_map(
        body, mesh=mesh, in_specs=placed, out_specs=(P("groups", AXES), P("groups", AXES)), check_vma=False
    )
```

```python
import functools

import jax
import jax.numpy as jnp
from jax import lax
from jax.experimental import pallas as pl
from jax.experimental.pallas import tpu as pltpu
from jax.sharding import PartitionSpec as P

M = 64
K = 32
NEAR = 5
NC = 3
NFAR = 8
HN = 2
HC = 2
LANES = 128
AXES = ("branch", "sub")
PIECES = 2
UNROLL = 32
FIRST = 1
CHUNK = 1024
F32 = jnp.float32
BF16 = jnp.bfloat16
NT = (((1,), (1,)), ((), ()))


def iota(shape, dim):
    return lax.broadcasted_iota(jnp.int32, shape, dim)


def place(node, count, levels):
    where = jnp.zeros_like(node)
    for level in range(levels):
        count //= 2
        where = where + (node & 1) * count
        node = node >> 1
    return where + node


def place_static(node, count, levels):
    where = 0
    for level in range(levels):
        count //= 2
        where += (node & 1) * count
        node >>= 1
    return where + node


def lane_order(count, levels, copies=1):
    rows = place(iota((count, count * copies), 0), count, levels)
    columns = iota((count, count * copies), 1) & (count - 1)
    return jnp.where(rows == columns, 1.0, 0.0).astype(BF16)


def dot(a, b):
    return jnp.dot(a, b, preferred_element_type=F32)


def end_nodes(count):
    return (0, 1, count - 2, count - 1)


def end_columns(count, offset):
    row, lane = iota((count, LANES), 0), iota((count, LANES), 1) & 7
    hit = row < 0
    for e, node in enumerate(end_nodes(count)):
        hit = hit | ((row == node) & (lane == offset + e))
    return jnp.where(hit, 1.0, 0.0).astype(BF16)


def rounded(x):
    return x.astype(BF16).astype(F32)


def contract(terms, init, lanes):
    def step(position, accs):
        for matrix_at, x_at in terms:
            matrix = matrix_at(position).astype(F32)
            accs = tuple(acc + matrix * x_at(r, position) for r, acc in enumerate(accs))
        return accs

    return lax.fori_loop(0, K, step, init, unroll=UNROLL)


def prep_up_kernel(first_ref, second_ref, third_ref, up1_ref, up2_ref, up3_ref):
    for source, target, levels, copies in ((first_ref, up1_ref, 3, 1), (second_ref, up2_ref, 2, 1), (third_ref, up3_ref, 1, 2)):
        count = source.shape[2]
        order = lane_order(count, levels, copies)
        for k in range(0, K, 4):
            rows = source[k : k + 4].reshape(4 * K, count)
            target[k : k + 4] = dot(rows, order).astype(BF16).reshape(4, K, count * copies)


def prep_rest_kernel(up1_ref, up2_ref, up3_ref, c1_ref, c2_ref, c3_ref, d1_ref, d2_ref, d3_ref, m1_ref, m2_ref, m3_ref, ends_ref, wide_ref):
    for source, target in ((up1_ref, d1_ref), (up2_ref, d2_ref), (up3_ref, d3_ref)):
        for tile in range(source.shape[2] // LANES):
            lanes = slice(tile * LANES, (tile + 1) * LANES)
            wide_ref[...] = source[:, :, lanes].astype(F32).reshape(K * K, LANES)
            for m in range(K):
                target[m, :, lanes] = wide_ref[pl.ds(m, K, stride=K), :].astype(BF16)
    for source, target, levels, copies in ((c1_ref, m1_ref, 2, 1), (c2_ref, m2_ref, 1, 2)):
        count = source.shape[3]
        order = lane_order(count, levels, copies)
        for j in range(NC):
            for k in range(0, K, 8):
                rows = source[j, k : k + 8].reshape(8 * K, count)
                target[j, k : k + 8] = dot(rows, order).astype(BF16).reshape(8, K, LANES)
    low_ends = end_columns(LANES, 0)
    high_ends = end_columns(M, 4)
    for j in range(NC):
        for k in range(0, K, 8):
            low = dot(c1_ref[j, k : k + 8].reshape(8 * K, LANES), low_ends)
            high = dot(c2_ref[j, k : k + 8].reshape(8 * K, M), high_ends)
            ends_ref[j, k : k + 8] = (low + high).astype(BF16).reshape(8, K, LANES)
    top = c3_ref.shape[3]
    group = LANES // top
    for h in range(NFAR // group):
        for k in range(0, K, 8):
            total = None
            for q in range(group):
                put = jnp.where(iota((top, LANES), 0) + q * top == iota((top, LANES), 1), 1.0, 0.0).astype(BF16)
                part = dot(c3_ref[h * group + q, k : k + 8].reshape(8 * K, top), put)
                total = part if total is None else total + part
            m3_ref[h, k : k + 8] = total.astype(BF16).reshape(8, K, LANES)


def spread_basis(part):
    low = iota((K, LANES), 1) < M
    zero = jnp.zeros((K, LANES), BF16)
    left, right = part[:, :LANES], part[:, LANES:]
    first = jnp.concatenate([jnp.where(low, left, zero), jnp.where(low, zero, left), zero, zero], axis=0)
    second = jnp.concatenate([zero, zero, jnp.where(low, right, zero), jnp.where(low, zero, right)], axis=0)
    return jnp.concatenate([first, second], axis=1)


def up_kernel(z_ref, basis_ref, up1_ref, up2_ref, up3_ref, sent_ref, coef1_ref, coef2_ref, rows_ref, x0_ref, x1_ref, x2_ref):
    rhs, order = z_ref.shape
    leaves = order // M
    top = leaves // 8
    groups = leaves // 4
    for g in range(groups):
        lanes = slice(g * 256, (g + 1) * 256)
        rows_ref[g * rhs : (g + 1) * rhs] = lax.dot_general(
            z_ref[:, lanes], spread_basis(basis_ref[:, lanes]), NT, preferred_element_type=F32
        )
    unit = jnp.where(iota((LANES, LANES), 0) == iota((LANES, LANES), 1), 1.0, 0.0).astype(BF16)
    for r in range(rhs):
        pieces = [rows_ref[pl.ds(a * rhs + r, top, stride=2 * rhs), :] for a in range(2)]
        flat = jnp.concatenate(pieces, axis=0).astype(BF16)
        both = jnp.concatenate([flat, flat], axis=0)
        tall = lax.dot_general(unit, both, NT, preferred_element_type=F32)
        keep = iota((K, LANES), 1) < M
        for c in range(2):
            x0_ref[c, r] = jnp.where(keep, tall[c * K : (c + 1) * K], tall[(2 + c) * K : (3 + c) * K])

    half = rhs // 2
    zeros = tuple(jnp.zeros((K, LANES), F32) for _ in range(half))
    for first in (0, half):
        terms = [
            (
                functools.partial(lambda s, k: up1_ref[k, :, s * LANES : (s + 1) * LANES], s),
                functools.partial(lambda s, r, k: x0_ref[s, first + r, pl.ds(k, 1), :], s),
            )
            for s in range(2)
        ]
        for r, acc in enumerate(contract(terms, zeros, LANES)):
            coef1_ref[first + r] = acc.astype(BF16)
            x1_ref[first + r] = rounded(acc)
    low = iota((K, LANES), 1) < M
    for first in (0, half):
        terms = [(lambda k: up2_ref[k], lambda r, k: x1_ref[first + r, pl.ds(k, 1), :])]
        for r, acc in enumerate(contract(terms, zeros, LANES)):
            total = rounded(acc + pltpu.roll(acc, 64, 1))
            if first == 0:
                x2_ref[r] = total
            else:
                both = jnp.where(low, x2_ref[r], total)
                x2_ref[r] = both
                coef2_ref[r] = both.astype(BF16)
    terms = [(lambda k: up3_ref[k], lambda r, k: x2_ref[r, pl.ds(k, 1), :])]
    sums = [acc + pltpu.roll(acc, 32, 1) for acc in contract(terms, zeros, LANES)]
    odd = (iota((K, LANES), 1) & 32) > 0
    for r in range(half // 2):
        sent_ref[r * K : (r + 1) * K] = jnp.where(odd, sums[r], pltpu.roll(sums[r + half // 2], 96, 1)).astype(BF16)

    def ends(count, offset, shift):
        row, column = iota((LANES, LANES), 0), iota((LANES, LANES), 1)
        hit = (row == -1)
        for copy in range(LANES // count):
            for e, node in enumerate((0, 1, count - 2, count - 1)):
                at = place_static(node, count, 2 if count == LANES else 1)
                hit = hit | ((row == copy * count + at) & (column == copy * M + offset + e))
        return jnp.where(hit, 1.0, 0.0).astype(BF16)

    first_ends = dot(x1_ref[...].astype(BF16).reshape(rhs * K, LANES), ends(LANES, 0, 0)).reshape(rhs, K, LANES)
    second_ends = dot(x2_ref[...].astype(BF16).reshape(half * K, LANES), ends(M, 4, 64)).reshape(half, K, LANES)
    packed = jnp.zeros((K, LANES), F32)
    for r in range(rhs):
        value = first_ends[r]
        if r < half:
            value = value + second_ends[r]
        packed = packed + (pltpu.roll(value, 8 * r, 1) if r else value)
    base = half // 2 * K
    sent_ref[base : base + K] = packed.astype(BF16)
    sent_ref[base + K : base + K + rhs] = z_ref[:, :LANES]
    sent_ref[base + K + rhs : base + K + 2 * rhs] = z_ref[:, order - LANES :]


def first_kernel(
    z_hbm, basis_hbm, first_hbm, second_hbm, third_hbm,
    sent_ref, coef1_ref, coef2_ref, up1_ref, up2_ref, up3_ref,
    z_ref, basis_ref, first_ref, second_ref, third_ref, sems, *scratch
):
    sources = (first_hbm, second_hbm, third_hbm, z_hbm, basis_hbm)
    targets = (first_ref, second_ref, third_ref, z_ref, basis_ref)
    copies = [pltpu.make_async_copy(a, b, sems.at[i]) for i, (a, b) in enumerate(zip(sources, targets))]
    for copy in copies:
        copy.start()
    for copy in copies[:3]:
        copy.wait()
    prep_up_kernel(first_ref, second_ref, third_ref, up1_ref, up2_ref, up3_ref)
    for copy in copies[3:]:
        copy.wait()
    up_kernel(z_ref, basis_ref, up1_ref, up2_ref, up3_ref, sent_ref, coef1_ref, coef2_ref, *scratch)


def put_leaves(target_ref, tile, slot):
    low = iota(tile.shape, 1) < M
    wide = tile.astype(F32)
    swapped = pltpu.roll(wide, M, 1)
    target_ref[slot] = jnp.where(low, wide, swapped).astype(BF16)
    target_ref[slot + 1] = jnp.where(low, swapped, wide).astype(BF16)


def own_blocks(res, rhs):
    low = iota((rhs, LANES), 1) < M
    return jnp.concatenate(
        [
            jnp.where(low, res[:rhs, :LANES], res[rhs : 2 * rhs, :LANES]),
            jnp.where(low, res[2 * rhs : 3 * rhs, LANES:], res[3 * rhs :, LANES:]),
        ],
        axis=1,
    )


def near_group(read, weights, rhs):
    low = iota((rhs, LANES), 1) < M
    rows = []
    for leaf in range(4):
        z = [read(j, leaf) for j in range(NEAR)]
        rows.append(jnp.concatenate([jnp.where(low, z[0], z[1]), jnp.where(low, z[2], z[3]), z[4][:, :M]], axis=1))
    return own_blocks(dot(jnp.concatenate(rows, axis=0), weights), rhs)


def near_kernel(chunk0, me_ref, leaves_ref, z_ref, blocks_ref, out_ref, z_leaves_ref):
    rhs, order = z_ref.shape
    chunks = out_ref.shape[1] // CHUNK
    per = CHUNK // M
    base = me_ref[0] * (order // M) - HN
    first_tile = max(chunk0 * (CHUNK // LANES) - 1, 0)
    last_tile = min((chunk0 + chunks) * (CHUNK // LANES) + 1, order // LANES)
    for t in range(first_tile, last_tile):
        put_leaves(z_leaves_ref, z_ref[:, t * LANES : (t + 1) * LANES], 2 * t + HN)

    @pl.loop(0, chunks)
    def _(c):
        for g in range(CHUNK // 256):
            leaf0 = (chunk0 + c) * per + 4 * g
            here = pl.ds(pl.multiple_of(c * CHUNK + g * 256, 256), 256)
            there = pl.ds(pl.multiple_of((chunk0 + c) * CHUNK + g * 256, 256), 256)
            weights = blocks_ref[:, :, there].reshape(NEAR * M, 256)
            out_ref[:, here] = near_group(lambda j, e: z_leaves_ref[leaves_ref[j, leaf0 + e] - base], weights, rhs)


def bit_reverse(value, bits):
    out = jnp.zeros_like(value)
    for b in range(bits):
        out = out + (((value >> b) & 1) << (bits - 1 - b))
    return out


def in_order(rows, count, levels):
    wide = jnp.concatenate([rows.astype(F32)] + [jnp.zeros((8 - rows.shape[0], count), F32)], axis=0).astype(BF16)
    return dot(wide, lane_order(count, levels)).astype(jnp.int32)


def own_rows_of(nodes, me, count, levels):
    local = nodes - me * count
    inside = (local >= 0) & (local < count)
    return in_order(jnp.where(inside, place(jnp.clip(local, 0, count - 1), count, levels), -1), count, levels)


def couple_kernel(
    bits, me_ref, coef1_ref, coef2_ref, list1_ref, list2_ref, top_ref, m1_ref, m2_ref, far1_ref, far2_ref, table_ref, picks_ref
):
    rhs, half = coef1_ref.shape[0], coef2_ref.shape[0]
    me = me_ref[0]
    devices, top = 1 << bits, top_ref.shape[1]
    per = LANES // top
    nodes = top_ref[...]
    rows = bit_reverse(jnp.bitwise_xor(nodes // top, me), bits) * top + nodes % top
    hot = []
    for j in range(NFAR):
        hot.append(jnp.where(iota((devices * top, top), 0) == rows[j : j + 1], 1.0, 0.0).astype(BF16))
    for h in range(NFAR // per):
        wide = None
        for q in range(per):
            put = jnp.where(iota((top, LANES), 0) + q * top == iota((top, LANES), 1), 1.0, 0.0).astype(BF16)
            part = dot(hot[h * per + q], put)
            wide = part if wide is None else wide + part
        table_ref[h] = wide.astype(BF16)
    zeros = tuple(jnp.zeros((K, LANES), F32) for _ in range(half))

    def run(matrix_ref, first):
        terms = [
            (
                functools.partial(lambda j, k: matrix_ref[j, k], j),
                functools.partial(lambda j, r, k: picks_ref[first + r, pl.ds(j * K + k, 1), :], j),
            )
            for j in range(NC)
        ]
        return contract(terms, zeros, LANES)

    rows = own_rows_of(list2_ref[...], me, M, 1)
    copy_of = iota((LANES, LANES), 1) // M
    tables = []
    for j in range(NC):
        row = jnp.concatenate([rows[j : j + 1], rows[j : j + 1]], axis=1)
        tables.append(jnp.where((iota((LANES, LANES), 0) - copy_of * M == row) & (row >= 0), 1.0, 0.0))
    table = jnp.concatenate(tables, axis=1).astype(BF16)
    picked = dot(coef2_ref[...].reshape(half * K, LANES), table).reshape(half, K, NC * LANES)
    for j in range(NC):
        picks_ref[:half, j * K : (j + 1) * K, :] = picked[:, :, j * LANES : (j + 1) * LANES]
    for r, acc in enumerate(run(m2_ref, 0)):
        far2_ref[r] = acc
    rows = own_rows_of(list1_ref[...], me, LANES, 2)
    table = jnp.concatenate(
        [jnp.where(iota((LANES, LANES), 0) == rows[j : j + 1], 1.0, 0.0) for j in range(NC)], axis=1
    ).astype(BF16)
    picked = dot(coef1_ref[...].reshape(rhs * K, LANES), table).reshape(rhs, K, NC * LANES)
    for j in range(NC):
        picks_ref[:, j * K : (j + 1) * K, :] = picked[:, :, j * LANES : (j + 1) * LANES]
    for first in (0, half):
        for r, acc in enumerate(run(m1_ref, first)):
            far1_ref[first + r] = acc


def halo_codes(nodes, me, count, offset):
    local = nodes - me * count
    code = jnp.where(local < 0, local + 5, jnp.where(local >= count, local - count + 1, 0))
    code = jnp.where(code > 0, code + offset, 0)
    wide = jnp.concatenate([code.astype(F32)] + [jnp.zeros((8 - code.shape[0], count), F32)], axis=0).astype(BF16)
    return dot(wide, end_columns(count, offset))


def down_kernel(bits, me_ref, leaves_ref, early_ref, late_ref, far1_in_ref, far2_in_ref, z_ref, *refs):
    near_refs = refs[:PIECES]
    (blocks_ref, basis_ref, list1_ref, list2_ref, table_ref, ends_ref, m3_ref, d1_ref, d2_ref, d3_ref,
     out_hbm, out_ref, every_ref, picks_ref, far1_ref, x_ref, x0_ref, rows_ref, z_leaves_ref, sems) = refs[PIECES:]
    rhs, order = z_ref.shape
    leaves = order // M
    top = leaves // 8
    half = rhs // 2
    me = me_ref[0]
    devices = 1 << bits
    own_rows = half // 2 * K

    def block(device, rows):
        at = bit_reverse(jnp.bitwise_xor(device, me), bits)
        early = early_ref[jnp.minimum(at, devices // 2 - 1), rows]
        late = late_ref[jnp.maximum(at - devices // 2, 0), rows]
        return jnp.where(at < devices // 2, early.astype(F32), late.astype(F32))

    before = jnp.maximum(me - 1, 0)
    after = jnp.minimum(me + 1, devices - 1)

    z_before = block(before, slice(own_rows + K + rhs, own_rows + K + 2 * rhs)).astype(BF16)
    z_after = block(after, slice(own_rows + K, own_rows + K + rhs)).astype(BF16)
    put_leaves(z_leaves_ref, z_before, 0)
    for t in range(3):
        put_leaves(z_leaves_ref, z_ref[:, t * LANES : (t + 1) * LANES], 2 + 2 * t)
        put_leaves(z_leaves_ref, z_ref[:, order - (3 - t) * LANES : order - (2 - t) * LANES or None], 8 + 2 * t)
    put_leaves(z_leaves_ref, z_after, 14)
    base = me * leaves - HN
    head = near_group(lambda j, e: z_leaves_ref[leaves_ref[j, e] - base], blocks_ref[:, :, :256].reshape(NEAR * M, 256), rhs)
    skip = leaves + 2 * HN - 16
    tail = near_group(
        lambda j, e: z_leaves_ref[leaves_ref[j, leaves - 4 + e] - base - skip], blocks_ref[:, :, order - 256 :].reshape(NEAR * M, 256), rhs
    )

    sides = slice(own_rows, own_rows + K)
    halo = jnp.where((iota((K, LANES), 1) & 2) > 0, block(before, sides), block(after, sides)).astype(BF16)
    codes = (halo_codes(list1_ref[...], me, LANES, 0) + halo_codes(list2_ref[...], me, M, 4)).astype(jnp.int32)
    lane_group = iota((LANES, LANES), 1) & -8
    sums = []
    for j in range(NC):
        code = codes[j : j + 1]
        table = jnp.where((iota((LANES, LANES), 0) == lane_group + code - 1) & (code > 0), 1.0, 0.0).astype(BF16)
        x_ref[j] = dot(halo, table)
    for j in range(NC):
        total = jnp.zeros((K, LANES), F32)
        for k in range(K):
            total = total + ends_ref[j, k].astype(F32) * x_ref[j, k : k + 1, :]
        sums.append(total)
    outer = sums[0] + sums[1] + sums[2]
    turned = jnp.concatenate([pltpu.roll(outer, LANES - 8 * r, 1) if r else outer for r in range(rhs)], axis=0)
    coarse = turned.astype(BF16)
    fine = (turned - coarse.astype(F32)).astype(BF16)

    def scatter(count, offset):
        row, column = iota((LANES, LANES), 0), iota((LANES, LANES), 1)
        hit = row < 0
        for copy in range(LANES // count):
            for e, node in enumerate(end_nodes(count)):
                at = place_static(node, count, 2 if count == LANES else 1)
                hit = hit | ((column == copy * count + at) & (row == copy * M + offset + e))
        return jnp.where(hit, 1.0, 0.0).astype(BF16)

    put = scatter(LANES, 0)
    outer1 = (dot(coarse, put) + dot(fine, put)).reshape(rhs, K, LANES)
    put = scatter(M, 4)
    outer2 = (dot(coarse[: half * K], put) + dot(fine[: half * K], put)).reshape(half, K, LANES)

    group = iota((own_rows, LANES), 1) // top
    per = LANES // top
    for tile in range(devices // per):
        source = early_ref if tile < devices // per // 2 else late_ref
        first = tile * per - (0 if tile < devices // per // 2 else devices // 2)
        parts = [source[first + q, :own_rows].astype(F32) for q in range(per)]
        for g in range(per):
            merged = None
            for q in range(per):
                shift = (q - g) * top % LANES
                moved = pltpu.roll(parts[q], shift, 1) if shift else parts[q]
                merged = moved if merged is None else jnp.where(group == q, moved, merged)
            every_ref[g * own_rows : (g + 1) * own_rows, tile * LANES : (tile + 1) * LANES] = merged.astype(BF16)
    for h in range(NFAR // per):
        picked = dot(every_ref[...], table_ref[h])
        picks_ref[:, h * K : (h + 1) * K, :] = picked.reshape(rhs, K, LANES)
    zeros = tuple(jnp.zeros((K, LANES), F32) for _ in range(half))
    groups_of = [1, 0, 3, 2]

    def slot(r):
        quarter = rhs // 4
        return groups_of[r // quarter] * quarter + r % quarter

    low = iota((K, LANES), 1) < M
    kept = {}
    for first in range(0, rhs, half):
        terms = [
            (
                functools.partial(lambda h, k: m3_ref[h, k], h),
                functools.partial(lambda h, r, k: picks_ref[slot(first + r), pl.ds(h * K + k, 1), :], h),
            )
            for h in range(NFAR // per)
        ]
        for r, acc in enumerate(contract(terms, zeros, LANES)):
            acc = acc + pltpu.roll(acc, 64, 1)
            acc = rounded(acc + pltpu.roll(acc, 32, 1))
            if first == 0:
                x_ref[r] = acc
            else:
                x_ref[r] = jnp.where(low, x_ref[r], acc)

    terms = [(lambda m: d3_ref[m], lambda r, m: x_ref[r, pl.ds(m, 1), :])]
    start = tuple(far2_in_ref[r] + outer2[r] for r in range(half))
    for r, acc in enumerate(contract(terms, start, LANES)):
        value = rounded(acc)
        swapped = pltpu.roll(value, M, 1)
        x_ref[r] = jnp.where(low, value, swapped)
        x_ref[r + half] = jnp.where(low, swapped, value)

    for first in (0, half):
        terms = [(lambda m: d2_ref[m], lambda r, m: x_ref[first + r, pl.ds(m, 1), :])]
        start = tuple(far1_in_ref[first + r] + outer1[first + r] for r in range(half))
        for r, acc in enumerate(contract(terms, start, LANES)):
            far1_ref[first + r] = rounded(acc)

    for first in (0, half):
        for s in range(2):
            lanes = slice(s * LANES, (s + 1) * LANES)
            terms = [(lambda m: d1_ref[m, :, lanes], lambda r, m: far1_ref[first + r, pl.ds(m, 1), :])]
            for r, acc in enumerate(contract(terms, zeros, LANES)):
                x0_ref[s, first + r] = acc
    groups = leaves // 4
    node = iota((LANES, LANES), 0) & (groups - 1)
    lane = (iota((LANES, LANES), 0) & -groups) + (node & 1) * top + (node >> 1)
    turn = jnp.where(lane == iota((LANES, LANES), 1), 1.0, 0.0).astype(BF16)
    for r in range(rhs):
        flat = jnp.concatenate([x0_ref[0, r], x0_ref[1, r]], axis=0).astype(BF16)
        both = jnp.concatenate([flat, flat], axis=0)
        tall = lax.dot_general(turn, both, NT, preferred_element_type=F32)
        keep = iota((groups, LANES), 1) < M
        rows_ref[pl.ds(r, groups, stride=rhs), :] = jnp.where(keep, tall[:groups], tall[groups:])

    def far_group(g):
        lanes = slice(g * 256, (g + 1) * 256)
        coefs = rows_ref[g * rhs : (g + 1) * rhs].astype(BF16)
        return dot(coefs, spread_basis(basis_ref[:, lanes]))

    total = leaves // 4
    parts = 4
    for part in range(parts):
        inside = range(part * total // parts, (part + 1) * total // parts)
        fars = [far_group(g) for g in inside]
        for g, far in zip(inside, fars):
            if g == 0:
                near = head
            elif g == total - 1:
                near = tail
            else:
                at = 0
                while g * 256 >= at + near_refs[0].shape[1]:
                    at += near_refs[0].shape[1]
                near = near_refs[at // near_refs[0].shape[1]][:, g * 256 - at : (g + 1) * 256 - at]
            out_ref[:, g * 256 : (g + 1) * 256] = (near + far).astype(BF16)
        lanes = slice(part * order // parts, (part + 1) * order // parts)
        pltpu.make_async_copy(out_ref.at[:, lanes], out_hbm.at[:, lanes], sems.at[part]).start()
    for part in range(parts):
        lanes = slice(part * order // parts, (part + 1) * order // parts)
        pltpu.make_async_copy(out_ref.at[:, lanes], out_hbm.at[:, lanes], sems.at[part]).wait()


VM = pl.BlockSpec(memory_space=pltpu.VMEM)
SM = pl.BlockSpec(memory_space=pltpu.SMEM)
HBM = pl.BlockSpec(memory_space=pltpu.HBM)


def params(mib):
    return pltpu.CompilerParams(vmem_limit_bytes=mib * 2**20)


def cost(flops, moved):
    return pl.CostEstimate(flops=flops, bytes_accessed=moved, transcendentals=0)


def shape(dims, kind=BF16):
    return jax.ShapeDtypeStruct(dims, kind)


def body(
    right_sides, near_blocks, near_leaves, leaf_basis, transfer_first, transfer_second, transfer_third,
    coupling_first, coupling_second, list_first, list_second, top_coupling, top_nodes,
):
    position = lax.axis_index(AXES)
    devices = lax.axis_size("branch") * lax.axis_size("sub")
    bits = devices.bit_length() - 1
    rhs, order = right_sides.shape
    leaves = order // M
    half = rhs // 2
    me = position.astype(jnp.int32).reshape(1)
    near_columns = near_leaves.T
    lists = (list_first.T, list_second.T, top_nodes.T)

    sent_rows = half // 2 * K + K + 2 * rhs
    up_shapes = (shape((sent_rows, LANES)), shape((rhs, K, LANES)), shape((half, K, LANES)))
    up_scratch = [
        pltpu.VMEM((leaves // 4 * rhs, LANES), F32),
        pltpu.VMEM((leaves // LANES, rhs, K, LANES), F32),
        pltpu.VMEM((rhs, K, LANES), F32),
        pltpu.VMEM((half, K, LANES), F32),
    ]
    *upward, up1, up2, up3 = pl.pallas_call(
        first_kernel,
        out_shape=up_shapes
        + (shape((K, K, leaves)), shape((K, K, LANES)), shape((K, K, LANES))),
        in_specs=[HBM] * 5,
        out_specs=(VM,) * 6,
        scratch_shapes=[
            pltpu.VMEM(a.shape, BF16)
            for a in (right_sides, leaf_basis, transfer_first, transfer_second, transfer_third)
        ]
        + [pltpu.SemaphoreType.DMA((5,))]
        + up_scratch,
        compiler_params=params(56),
        cost_estimate=cost(FIRST * 10**9, 3 * 2**20),
    )(right_sides, leaf_basis, transfer_first, transfer_second, transfer_third)
    vectors, basis, blocks = right_sides, leaf_basis, near_blocks
    cut = order // PIECES

    def prepare(up1, up2, up3):
        return pl.pallas_call(
            prep_rest_kernel,
            out_shape=(
                shape((K, K, leaves)), shape((K, K, LANES)), shape((K, K, LANES)),
                shape((NC, K, K, LANES)), shape((NC, K, K, LANES)),
                shape((NFAR * top_coupling.shape[3] // LANES, K, K, LANES)), shape((NC, K, K, LANES)),
            ),
            in_specs=[VM] * 6,
            out_specs=(VM,) * 7,
            scratch_shapes=[pltpu.VMEM((K * K, LANES), F32)],
            compiler_params=params(16),
            cost_estimate=cost(10**9, 9 * 2**20),
        )(up1, up2, up3, coupling_first, coupling_second, top_coupling)

    def near_piece(i, vectors):
        return pl.pallas_call(
            functools.partial(near_kernel, i * cut // CHUNK),
            out_shape=shape((rhs, cut), F32),
            in_specs=[SM, SM, VM, VM],
            out_specs=VM,
            scratch_shapes=[pltpu.VMEM((leaves + 2 * HN, rhs, LANES), BF16)],
            compiler_params=params(16),
            cost_estimate=cost(10**9, 8 * 2**20),
        )(me, near_columns, vectors, blocks)

    def couple(coef1, coef2, m1, m2):
        return pl.pallas_call(
            functools.partial(couple_kernel, bits),
            out_shape=(
                shape((rhs, K, LANES), F32), shape((half, K, LANES), F32),
                shape((NFAR * (leaves // 8) // LANES, devices * (leaves // 8), LANES)),
            ),
            in_specs=[SM] + [VM] * 7,
            out_specs=(VM,) * 3,
            scratch_shapes=[pltpu.VMEM((rhs, NC * K, LANES), F32)],
            compiler_params=params(16),
            cost_estimate=cost(10**9, 8 * 2**20),
        )(me, coef1, coef2, *lists, m1, m2)

    def exchange(sent, works):
        every, done = sent[None], []
        for step, b in enumerate(reversed(range(bits))):
            pairs = [(i, i ^ (1 << b)) for i in range(devices)]
            other = lax.ppermute(every, AXES, pairs)
            if step < len(works):
                result = works[step](every)
                other, result = lax.optimization_barrier((other, result))
                done.append(result)
            if b:
                every = jnp.concatenate([every, other], axis=0)
        return every, other, done

    def held(values, every):
        return lax.optimization_barrier((*values, every))[:-1]

    def down(every, other, far1, far2, table, vectors, nears, prepared, keep):
        d1, d2, d3, _, _, m3, ends = prepared
        out = shape((rhs, order))
        results = pl.pallas_call(
            functools.partial(down_kernel, bits),
            out_shape=(out, out) if keep else (out,),
            in_specs=[SM, SM] + [VM] * 5 + [VM] * PIECES + [VM] * 10,
            out_specs=(HBM, VM) if keep else (HBM,),
            scratch_shapes=([] if keep else [pltpu.VMEM((rhs, order), BF16)])
            + [
                pltpu.VMEM((rhs * K, devices * (leaves // 8)), BF16),
                pltpu.VMEM((rhs, NFAR * K * (leaves // 8) // LANES, LANES), F32),
                pltpu.VMEM((rhs, K, LANES), F32),
                pltpu.VMEM((rhs, K, LANES), F32),
                pltpu.VMEM((leaves // LANES, rhs, K, LANES), F32),
                pltpu.VMEM((leaves // 4 * rhs, LANES), F32),
                pltpu.VMEM((16, rhs, LANES), BF16),
                pltpu.SemaphoreType.DMA((4,)),
            ],
            compiler_params=params(24),
            cost_estimate=cost(10**9, 8 * 2**20),
        )(me, near_columns, every, other, far1, far2, vectors, *nears, blocks, basis, *lists[:2], table, ends, m3, d1, d2, d3)
        return results

    sent, coef1, coef2 = upward
    prepared = []
    works = [
        lambda every: near_piece(0, *held((vectors,), every)),
        lambda every: prepared.extend(prepare(*held((up1, up2, up3), every))) or tuple(prepared),
        lambda every: couple(*held((coef1, coef2), every), *prepared[3:5]),
        lambda every: near_piece(1, *held((vectors,), every)),
    ]
    every, other, (near0, prepared, fars, near1) = exchange(sent, works)
    first_image, second_vectors = down(every, other, *fars, vectors, (near0, near1), prepared, True)
    sent, coef1, coef2 = pl.pallas_call(
        up_kernel,
        out_shape=up_shapes,
        in_specs=[VM] * 5,
        out_specs=(VM,) * 3,
        scratch_shapes=up_scratch,
        compiler_params=params(12),
        cost_estimate=cost(10**8, 3 * 2**20),
    )(second_vectors, basis, up1, up2, up3)
    works = [
        lambda every: couple(*held((coef1, coef2), every), *prepared[3:5]),
        lambda every: near_piece(0, *held((second_vectors,), every)),
        lambda every: near_piece(1, *held((second_vectors,), every)),
    ]
    every, other, (fars, near0, near1) = exchange(sent, works)
    (second_image,) = down(every, other, *fars, second_vectors, (near0, near1), prepared, False)
    return (first_image, second_image)


def solution(mesh):
    tree = P(None, None, AXES)
    placed = (
        P("groups", AXES), tree, P(AXES, None), P(None, AXES), tree, tree, tree,
        P(None, None, None, AXES), P(None, None, None, AXES), P(AXES, None), P(AXES, None),
        P(None, None, None, AXES), P(AXES, None),
    )
    return jax.shard_map(
        body, mesh=mesh, in_specs=placed, out_specs=(P("groups", AXES), P("groups", AXES)), check_vma=False
    )
```
